128 devices in a mesh: seq: 16 (over y, z_lo, core), chan: 8 (over z_hi, x).
Axes of the slice: x: 4, y: 4, z: 4 (z_hi: 2, z_lo: 2; z = z_hi * 2 + z_lo), core: 2. Of those that a mesh axis runs over, the one named last changes fastest.
Arguments:
- stream_one: bfloat16 [4096, 8192], P('chan', 'seq'), may hold values from -6 to 6
- stream_two: bfloat16 [4096, 8192], P('chan', 'seq'), may hold values from -6 to 6
- stream_value: bfloat16 [4096, 8192], P('chan', 'seq'), may hold values from -6 to 6
- grad_output: bfloat16 [4096, 8192], P('chan', 'seq'), may hold values from -6 to 6
- long_taps: bfloat16 [4096, 8192], P('chan', 'seq'), may hold values from -0.0625 to 0.0625
- short_taps: float32 [3, 3, 4096], P(None, None, 'chan'), may hold values from -3.5 to 3.5
- skip_gain: float32 [4096], P('chan'), may hold values from 0.25 to 1.5
- sketch_matrix: bfloat16 [1024, 8192], P(None, 'seq'), may hold values from -0.0007324219 to 0.0007324219
Outputs:
- grad_one: bfloat16 [4096, 8192], P('chan', 'seq')
- grad_two: bfloat16 [4096, 8192], P('chan', 'seq')
- grad_value: bfloat16 [4096, 8192], P('chan', 'seq')
- saliency: float32 [8192], P(('seq', 'chan'))
- sketch: float32 [1024, 4096], P('seq', 'chan')
The draws below stay inside these ranges and needn't reach their ends.
All inputs are finite; a program needn't handle non-finite values.
Results may differ from the reference program's by a relative error of at most 0.0057.
Values may be sent and summed in bfloat16 or wider, within the bound.
A program may use at most 128 MiB of HBM per device.

```python
import jax
import jax.numpy as jnp
from jax import lax

D = 4096
K = 1024
LEN = 8192


def levels(rng, extent, pieces, least, high):
    gain, own = 1.0, jax.random.fold_in(rng, 6)
    for dim, parts in pieces:
        steps = jnp.exp(jax.random.uniform(jax.random.fold_in(own, dim), (parts,), jnp.float32, least / len(pieces), high / len(pieces)))
        gain = gain * jnp.repeat(steps, extent[dim] // parts).reshape([-1 if axis == dim else 1 for axis in range(len(extent))])
    return gain


def centred(key, extent, spread, bound, cuts=(), held_as=jnp.bfloat16):
    values = jax.random.normal(key, extent, jnp.float32) * spread
    if len(cuts) > 0:
        values = levels(key, extent, cuts, -0.22, 0.18) * values
    return jnp.clip(values, min=-bound, max=bound).astype(held_as)


def setup_inputs(seed: int = 0) -> dict:
    arg_keys = jax.random.split(jax.random.key(seed), 9)
    stream_one = centred(arg_keys[0], (D, LEN), 1.0, 6.0, ((0, 8), (1, 16)))
    stream_two = centred(arg_keys[1], (D, LEN), 1.0, 6.0, ((0, 8), (1, 16)))
    stream_value = centred(arg_keys[2], (D, LEN), 1.0, 6.0, ((0, 8), (1, 16)))
    grad_output = centred(arg_keys[3], (D, LEN), 1.0, 6.0, ((0, 8), (1, 16)))
    long_taps = centred(arg_keys[4], (D, LEN), LEN ** -0.5, 0.0625, ((0, 8), (1, 16)))
    short_taps = centred(arg_keys[5], (3, 3, D), 3 ** -0.5, 3.5, ((2, 8),), jnp.float32)
    skip_gain = jnp.clip(0.25 + 1.25 * jax.random.uniform(arg_keys[6], (D,), jnp.float32) ** levels(arg_keys[6], (D,), ((0, 8),), -0.2, 0.2), 0.25, 1.5)
    sketch_matrix = centred(arg_keys[7], (K, LEN), (LEN * LEN) ** -0.5, 0.0007324219, ((1, 16),))
    return {"stream_one": stream_one, "stream_two": stream_two, "stream_value": stream_value, "grad_output": grad_output, "long_taps": long_taps, "short_taps": short_taps, "skip_gain": skip_gain, "sketch_matrix": sketch_matrix}


def delay(field, steps):
    return jnp.pad(field[:, :field.shape[1] - steps], ((0, 0), (steps, 0)))


def advance(field, steps):
    return jnp.pad(field[:, steps:], ((0, 0), (0, steps)))


def causal_short(field, weights):
    return weights[0][:, None] * field + weights[1][:, None] * delay(field, 1) + weights[2][:, None] * delay(field, 2)


def adjoint_short(field, weights):
    return weights[0][:, None] * field + weights[1][:, None] * advance(field, 1) + weights[2][:, None] * advance(field, 2)


def channel_block(items):
    stream_one, stream_two, stream_value, grad_output, long_taps, conv_taps, gains = items
    length = stream_one.shape[1]
    padded = 2 * length
    first_in = stream_one.astype(jnp.float32)
    second_in = stream_two.astype(jnp.float32)
    value_in = stream_value.astype(jnp.float32)
    grad_in = grad_output.astype(jnp.float32)
    act_one = causal_short(first_in, conv_taps[0])
    act_two = causal_short(second_in, conv_taps[1])
    act_value = causal_short(value_in, conv_taps[2])
    gated = (act_two * act_value).astype(jnp.bfloat16)
    gated_wide = lax.optimization_barrier(gated).astype(jnp.float32)
    grad_gate = (grad_in * act_one).astype(jnp.bfloat16)
    grad_gate_wide = lax.optimization_barrier(grad_gate).astype(jnp.float32)
    spec_filter = jnp.fft.rfft(long_taps.astype(jnp.float32), n=padded, axis=1)
    spec_gate = jnp.fft.rfft(gated_wide, n=padded, axis=1)
    spec_grad = jnp.fft.rfft(grad_gate_wide, n=padded, axis=1)
    mixed = jnp.fft.irfft(spec_filter * spec_gate, n=padded, axis=1)[:, :length] + gains[:, None] * gated_wide
    grad_mix = jnp.fft.irfft(jnp.conj(spec_filter) * spec_grad, n=padded, axis=1)[:, :length] + gains[:, None] * grad_gate_wide
    grad_filter = jnp.fft.irfft(jnp.conj(spec_gate) * spec_grad, n=padded, axis=1)[:, :length].astype(jnp.bfloat16)
    full_one = adjoint_short(grad_in * mixed, conv_taps[0])
    full_two = adjoint_short(grad_mix * act_value, conv_taps[1])
    full_value = adjoint_short(grad_mix * act_two, conv_taps[2])
    attrib = jnp.sum(first_in * full_one + second_in * full_two + value_in * full_value, axis=0)
    return (full_one.astype(jnp.bfloat16), full_two.astype(jnp.bfloat16), full_value.astype(jnp.bfloat16), grad_filter, attrib)


def reference(stream_one, stream_two, stream_value, grad_output, long_taps, short_taps, skip_gain, sketch_matrix):
    block = 128
    count = D // block

    def fold(field):
        return field.reshape(count, block, LEN)

    conv_taps = jnp.moveaxis(short_taps.reshape(3, 3, count, block), 2, 0)
    gains = skip_gain.reshape(count, block)
    results = lax.map(channel_block, (fold(stream_one), fold(stream_two), fold(stream_value), fold(grad_output), fold(long_taps), conv_taps, gains))
    grad_one = results[0].reshape(D, LEN)
    grad_two = results[1].reshape(D, LEN)
    grad_value = results[2].reshape(D, LEN)
    grad_filter = results[3].reshape(D, LEN)
    saliency = jnp.sum(results[4], axis=0) * (3.0 * D) ** -0.5
    sketch = jnp.dot(sketch_matrix, grad_filter.T, preferred_element_type=jnp.float32)
    return (grad_one, grad_two, grad_value, saliency, sketch)
```

```python
import functools
import math

import jax
import jax.numpy as jnp
import numpy as np
from jax import lax
from jax.experimental import pallas as pl
from jax.experimental.pallas import tpu as pltpu
from jax.sharding import PartitionSpec as P

D = 4096
MESH = pl.DeviceIdType.MESH
F32 = jnp.float32
BF16 = jnp.bfloat16
ROOT = math.sqrt(0.5)
FREQS = [k1 + 32 * q for k1 in range(1, 16) for q in range(4)] + [0, 32, 64, 16, 48]
ROWS = 32 * len(FREQS)
CHUNK = 416


def split_host(table):
    high = table.astype(jnp.bfloat16)
    low = (table - high.astype(np.float64)).astype(jnp.bfloat16)
    return high, low


def host_tables():
    shard = np.arange(16)
    k1 = np.arange(16)
    first = np.zeros((4, 32, 16))
    for tile in range(4):
        angle = 2 * np.pi * np.outer(k1, 4 * shard + tile) / 128
        first[tile, :16] = np.cos(angle)
        first[tile, 16:] = -np.sin(angle)
        first[tile, 16] = (-1.0) ** shard
    eye = np.eye(16)
    wide = np.einsum("tks,cd->tkcsd", first, eye).reshape(4, 512, 256)
    back = np.einsum("tks,cd->tsckd", first, eye).reshape(4, 256, 512) * (2.0 / 16384)
    lane = np.arange(128)
    angle = 2 * np.pi * np.outer(lane, lane) / 128
    cos, sin = np.cos(angle), np.sin(angle)
    inner = np.block([[cos, -sin], [sin, cos]])
    inner_back = np.block([[cos, sin], [-sin, cos]])
    twist = 2 * np.pi * np.outer(np.array(FREQS + [0] * 7), lane) / 16384
    twist = np.concatenate([twist, twist], axis=1)
    return (
        *split_host(wide),
        *split_host(back),
        *split_host(inner),
        *split_host(inner_back),
        np.cos(twist).astype(np.float32),
        np.sin(twist).astype(np.float32),
    )


def dot(left, right):
    return jnp.dot(left, right, preferred_element_type=F32)


def dot_nt(left, right):
    return lax.dot_general(left, right, (((1,), (1,)), ((), ())), preferred_element_type=F32)


def halves(value):
    high = value.astype(BF16)
    return high, (value - high.astype(F32)).astype(BF16)


def loop(first, last, body):
    def step(index, carry):
        body(index)
        return carry

    lax.fori_loop(first, last, step, 0)


def kernel(
    x1_h, x2_h, xv_h, go_h, taps_h, short_h, gain_h, sk_h,
    c1h_h, c1l_h, dh_h, dl_h, mh_h, ml_h, nh_h, nl_h, twc_h, tws_h,
    o1_h, o2_h, ov_h, osal_h, osk_h,
    x1, x2, xv, go, short, gain, sk,
    c1h, c1l, dh, dl, mh, ml, nh, nl, twc, tws,
    wrow, wcol, tail_s, tail_r, edge_s, edge_r, hcol,
    gg_s, g_s, act2, actv,
    taps_r, gg_r, g_r,
    y, zh, zl, spec_t, spec_b, spec_a, e, wh, wl,
    gf_s, mix_s, gmix_s, gf_r, mix_r, gmix_r,
    part_s, rs_r, ga1, ga2, gav, sal_s, sal_r, o1, o2, ov, osal, osk,
    load_sem, self_sem, out_sem, send_sem, recv_sem, halo_send, halo_recv, sal_send, sal_recv,
):
    me = lax.axis_index("seq")
    chan = lax.axis_index("chan")
    core = lax.rem(me, 2)
    half = me // 8
    sibling = me + 1 - 2 * core
    following = lax.rem(me + 1, 16)
    previous = lax.rem(me + 15, 16)

    loads = [
        (x1_h, x1), (x2_h, x2), (xv_h, xv), (go_h, go), (short_h, short), (gain_h, gain),
        (c1h_h, c1h), (c1l_h, c1l), (mh_h, mh), (ml_h, ml), (twc_h, twc), (tws_h, tws),
        (nh_h, nh), (nl_h, nl), (dh_h, dh), (dl_h, dl), (sk_h, sk.at[core]),
    ]
    loads = [pltpu.make_async_copy(a, b, load_sem.at[n]) for n, (a, b) in enumerate(loads)]
    for load in loads:
        load.start()

    barrier = pltpu.get_barrier_semaphore()
    loop(1, 16, lambda i: pl.semaphore_signal(
        barrier, inc=1, device_id=(lax.rem(me + i, 16), chan), device_id_type=MESH))
    loop(1, 8, lambda i: pl.semaphore_signal(
        barrier, inc=1, device_id=(me, lax.rem(chan + i, 8)), device_id_type=MESH))

    def block_of(ref):
        return lambda to: ref.at[pl.ds(pl.multiple_of(to * 32, 32), 32)]

    def slot_of(ref):
        return lambda to: ref.at[to]

    def start_send(kind, source, target, first=1, last=16):
        def one(i):
            to = lax.rem(me + i, 16)
            pltpu.make_async_remote_copy(
                src_ref=source(to), dst_ref=target.at[me],
                send_sem=send_sem.at[kind, i], recv_sem=recv_sem.at[kind, i],
                device_id=(to, chan), device_id_type=MESH,
            ).start()

        loop(first, last, one)

    def wait_arrived(kind, source, target):
        def one(i):
            origin = lax.rem(me + 16 - i, 16)
            pltpu.make_async_remote_copy(
                src_ref=source(origin), dst_ref=target.at[origin],
                send_sem=send_sem.at[kind, i], recv_sem=recv_sem.at[kind, i],
                device_id=(origin, chan), device_id_type=MESH,
            ).wait_recv()

        loop(1, 16, one)

    def wait_sent(kind, source, target):
        def one(i):
            to = lax.rem(me + i, 16)
            pltpu.make_async_remote_copy(
                src_ref=source(to), dst_ref=target.at[me],
                send_sem=send_sem.at[kind, i], recv_sem=recv_sem.at[kind, i],
                device_id=(to, chan), device_id_type=MESH,
            ).wait_send()

        loop(1, 16, one)

    def own(kind, source, target):
        return pltpu.make_async_copy(source(me), target.at[me], self_sem.at[kind])

    def neighbour(source, target, n, to):
        return pltpu.make_async_remote_copy(
            src_ref=source, dst_ref=target, send_sem=halo_send.at[n], recv_sem=halo_recv.at[n],
            device_id=(to, chan), device_id_type=MESH)

    for n in range(6):
        loads[n].wait()
    row = lax.broadcasted_iota(jnp.int32, (16, 128), 0)
    lane = lax.broadcasted_iota(jnp.int32, (16, 128), 1)
    tails = jnp.zeros((16, 512), F32)
    for s, ref in enumerate((x1, x2, xv)):
        pick = ((row == 2 * s) & (lane == 126)) | ((row == 2 * s + 1) & (lane == 127))
        tails += dot_nt(pick.astype(F32).astype(BF16), ref[:, 384:512])
    tail_s[...] = tails.astype(BF16)

    pl.semaphore_wait(barrier, 22)
    tail_copy = neighbour(tail_s, tail_r, 0, following)
    tail_copy.start()
    start_send(0, block_of(taps_h), taps_r, 1, 7)
    own(0, block_of(taps_h), taps_r).start()

    wrow[...] = jnp.zeros((128, 512), F32)
    for s in range(3):
        wrow[3 * s : 3 * s + 3, :] = short[s]
    wrow[9:10, :] = gain[...]
    wcol[...] = jnp.transpose(wrow[...])

    tail_copy.wait_recv()
    wrow[0:16, :] = tail_r[...].astype(F32) * (me > 0).astype(F32)
    hcol[...] = jnp.transpose(wrow[...])

    lane32 = lax.broadcasted_iota(jnp.int32, (32, 512), 1)

    def gate(block):
        rows = pl.ds(pl.multiple_of(block * 32, 32), 32)
        weight = wcol[rows, :]
        halo = hcol[rows, :]

        def short_filter(ref, s):
            field = ref[rows, :].astype(F32)
            before, last = halo[:, 2 * s : 2 * s + 1], halo[:, 2 * s + 1 : 2 * s + 2]
            one = jnp.where(lane32 == 0, last, pltpu.roll(field, 1, 1))
            two = jnp.where(lane32 == 0, before, jnp.where(lane32 == 1, last, pltpu.roll(field, 2, 1)))
            return (
                weight[:, 3 * s : 3 * s + 1] * field
                + weight[:, 3 * s + 1 : 3 * s + 2] * one
                + weight[:, 3 * s + 2 : 3 * s + 3] * two
            )

        first = short_filter(x1, 0)
        gg_s[rows, :] = (go[rows, :].astype(F32) * first).astype(BF16)
        second = short_filter(x2, 1)
        value = short_filter(xv, 2)
        act2[rows, :] = second
        actv[rows, :] = value
        g_s[rows, :] = (second * value).astype(BF16)

    loop(0, 16, gate)
    start_send(1, block_of(gg_s), gg_r)
    own(1, block_of(gg_s), gg_r).start()
    start_send(2, block_of(g_s), g_r)
    own(2, block_of(g_s), g_r).start()
    start_send(0, block_of(taps_h), taps_r, 7, 16)
    swap = neighbour(sk_h, sk.at[core], 2, sibling)
    swap.start()

    def first_rows(tile, part, k1):
        return y[tile, pl.ds(pl.multiple_of(part * 256 + k1 * 16, 16), 16), :]

    def store_z(index, re, im):
        for g in range(2):
            rows = pl.ds(pl.multiple_of(index * 32 + g * 16, 16), 16)
            side = slice(g * 128, g * 128 + 128)
            high, low = halves(jnp.concatenate([re[:, side], im[:, side]], axis=1))
            zh[rows, :] = high
            zl[rows, :] = low

    def twist(index, re, im):
        cos, sin = twc[pl.ds(index, 1), :], tws[pl.ds(index, 1), :]
        store_z(index, re * cos + im * sin, im * cos - re * sin)

    def forward(source, spec):
        def stage(tile):
            lanes = pl.ds(pl.multiple_of(tile * 128, 128), 128)
            right = jnp.concatenate(
                [source[:, 0:16, lanes].reshape(256, 128), source[:, 16:32, lanes].reshape(256, 128)],
                axis=1)
            y[tile] = dot(c1h[tile], right) + dot(c1l[tile], right)

        loop(0, 4, stage)

        def butterfly(k1):
            r0, r1, r2, r3 = [first_rows(t, 0, k1) for t in range(4)]
            i0, i1, i2, i3 = [first_rows(t, 1, k1) for t in range(4)]
            ar, ai, br, bi = r0 + r2, i0 + i2, r0 - r2, i0 - i2
            cr, ci, dr, di = r1 + r3, i1 + i3, r1 - r3, i1 - i3
            base = (k1 - 1) * 4
            twist(base, ar + cr, ai + ci)
            twist(base + 1, br + di, bi - dr)
            twist(base + 2, ar - cr, ai - ci)
            twist(base + 3, br - di, bi + dr)

        loop(1, 16, butterfly)
        r0, r1, r2, r3 = [first_rows(t, 0, 0) for t in range(4)]
        none = jnp.zeros_like(r0)
        store_z(60, r0 + r1 + r2 + r3, none)
        twist(61, r0 - r2, r3 - r1)
        twist(62, r0 - r1 + r2 - r3, none)
        r0, r1, r2, r3 = [first_rows(t, 1, 0) for t in range(4)]
        twist(63, r0 + ROOT * (r1 - r3), -r2 - ROOT * (r1 + r3))
        twist(64, r0 - ROOT * (r1 - r3), r2 - ROOT * (r1 + r3))

        def last(chunk):
            rows = pl.ds(pl.multiple_of(chunk * CHUNK, 16), CHUNK)
            spec[rows, :] = dot(zh[rows, :], mh[...]) + dot(zl[rows, :], mh[...]) + dot(zh[rows, :], ml[...])

        loop(0, ROWS // CHUNK, last)

    def inverse(spec_l, spec_r, conj, target):
        sign = -1.0 if conj else 1.0

        def first(chunk):
            rows = pl.ds(pl.multiple_of(chunk * CHUNK, 16), CHUNK)
            lr, li = spec_l[rows, 0:128], spec_l[rows, 128:256] * sign
            rr, ri = spec_r[rows, 0:128], spec_r[rows, 128:256]
            high, low = halves(jnp.concatenate([lr * rr - li * ri, lr * ri + li * rr], axis=1))
            e[rows, :] = dot(high, nh[...]) + dot(low, nh[...]) + dot(high, nl[...])

        loop(0, ROWS // CHUNK, first)

        def untwist(index):
            cos, sin = twc[pl.ds(index, 1), :], tws[pl.ds(index, 1), :]
            top = e[pl.ds(pl.multiple_of(index * 32, 32), 16), :]
            low = e[pl.ds(pl.multiple_of(index * 32 + 16, 16), 16), :]
            re = jnp.concatenate([top[:, 0:128], low[:, 0:128]], axis=1)
            im = jnp.concatenate([top[:, 128:256], low[:, 128:256]], axis=1)
            return re * cos - im * sin, im * cos + re * sin

        def store_w(tile, part, k1, value):
            rows = pl.ds(pl.multiple_of(part * 256 + k1 * 16, 16), 16)
            high, low = halves(value)
            wh[tile, rows, :] = high
            wl[tile, rows, :] = low

        def butterfly(k1):
            base = (k1 - 1) * 4
            (r0, i0), (r1, i1), (r2, i2), (r3, i3) = [untwist(base + q) for q in range(4)]
            ar, ai, br, bi = r0 + r2, i0 + i2, r0 - r2, i0 - i2
            cr, ci, dr, di = r1 + r3, i1 + i3, r1 - r3, i1 - i3
            store_w(0, 0, k1, ar + cr)
            store_w(0, 1, k1, ai + ci)
            store_w(1, 0, k1, br - di)
            store_w(1, 1, k1, bi + dr)
            store_w(2, 0, k1, ar - cr)
            store_w(2, 1, k1, ai - ci)
            store_w(3, 0, k1, br + di)
            store_w(3, 1, k1, bi - dr)

        loop(1, 16, butterfly)
        (r0, _), (r32, i32), (r64, _), (r16, i16), (r48, i48) = [untwist(60 + n) for n in range(5)]
        plus, minus = 0.5 * (r0 + r64), 0.5 * (r0 - r64)
        store_w(0, 0, 0, plus + r32)
        store_w(1, 0, 0, minus - i32)
        store_w(2, 0, 0, plus - r32)
        store_w(3, 0, 0, minus + i32)
        store_w(0, 1, 0, r16 + r48)
        store_w(1, 1, 0, ROOT * (r16 - i16 - r48 - i48))
        store_w(2, 1, 0, i48 - i16)
        store_w(3, 1, 0, ROOT * (r48 - i48 - r16 - i16))

        def last(tile):
            lanes = pl.ds(pl.multiple_of(tile * 128, 128), 128)
            out = dot(dh[tile], wh[tile]) + dot(dh[tile], wl[tile]) + dot(dl[tile], wh[tile])
            out = out.astype(BF16)
            target[:, 0:16, lanes] = out[:, 0:128].reshape(16, 16, 128)
            target[:, 16:32, lanes] = out[:, 128:256].reshape(16, 16, 128)

        loop(0, 4, last)

    for n in range(6, 16):
        loads[n].wait()
    own(1, block_of(gg_s), gg_r).wait()
    wait_arrived(1, block_of(gg_s), gg_r)
    forward(gg_r, spec_b)
    own(2, block_of(g_s), g_r).wait()
    wait_arrived(2, block_of(g_s), g_r)
    forward(g_r, spec_a)
    inverse(spec_a, spec_b, True, gf_s)

    def filter_source(chip):
        return gf_s.at[pl.ds(2 * chip, 2)]

    def filter_copy(chip):
        to = 2 * chip + half
        return pltpu.make_async_remote_copy(
            src_ref=filter_source(chip), dst_ref=gf_r.at[me - 8 * half],
            send_sem=send_sem.at[3, chip], recv_sem=recv_sem.at[3, me - 8 * half],
            device_id=(to, chan), device_id_type=MESH)

    def filter_own():
        return pltpu.make_async_copy(
            filter_source(me // 2), gf_r.at[me - 8 * half], self_sem.at[3])

    def send_filter(n):
        chip = lax.rem(me // 2 + n, 8)

        @pl.when(2 * chip + half != me)
        def _():
            filter_copy(chip).start()

    loop(0, 8, send_filter)

    @pl.when(core == half)
    def _():
        filter_own().start()

    own(0, block_of(taps_h), taps_r).wait()
    wait_arrived(0, block_of(taps_h), taps_r)
    forward(taps_r, spec_t)
    inverse(spec_t, spec_a, False, mix_s)
    start_send(4, slot_of(mix_s), mix_r)
    own(4, slot_of(mix_s), mix_r).start()
    inverse(spec_t, spec_b, True, gmix_s)
    start_send(5, slot_of(gmix_s), gmix_r)
    own(5, slot_of(gmix_s), gmix_r).start()

    loads[16].wait()
    swap_in = neighbour(sk_h, sk.at[1 - core], 2, sibling)
    swap_in.wait_recv()

    @pl.when(core == half)
    def _():
        filter_own().wait()

    def filter_arrived(n):
        origin = 8 * core + n

        @pl.when(origin != me)
        def _():
            pltpu.make_async_remote_copy(
                src_ref=filter_source(0), dst_ref=gf_r.at[n],
                send_sem=send_sem.at[3, 0], recv_sem=recv_sem.at[3, n],
                device_id=(origin, chan), device_id_type=MESH).wait_recv()

    loop(0, 8, filter_arrived)

    def sketch_rows(block):
        rows = pl.ds(pl.multiple_of(block * 256, 256), 256)
        total = dot_nt(sk[0, rows, :], gf_r[:, 0].reshape(256, 512))
        total += dot_nt(sk[1, rows, :], gf_r[:, 1].reshape(256, 512))
        part_s[pl.ds(block * 4, 4)] = total.astype(BF16).reshape(4, 64, 256)

    loop(0, 4, sketch_rows)
    start_send(6, slot_of(part_s), rs_r)
    own(6, slot_of(part_s), rs_r).start()

    own(4, slot_of(mix_s), mix_r).wait()
    wait_arrived(4, slot_of(mix_s), mix_r)
    own(5, slot_of(gmix_s), gmix_r).wait()
    wait_arrived(5, slot_of(gmix_s), gmix_r)

    def activations(block):
        rows = pl.ds(pl.multiple_of(block * 32, 32), 32)
        skip = wcol[rows, 9:10]
        mixed = mix_r[block].astype(F32) + skip * g_s[rows, :].astype(F32)
        ga1[rows, :] = go[rows, :].astype(F32) * mixed
        grad_mix = gmix_r[block].astype(F32) + skip * gg_s[rows, :].astype(F32)
        ga2[rows, :] = grad_mix * actv[rows, :]
        gav[rows, :] = grad_mix * act2[rows, :]

    loop(0, 16, activations)
    edges = jnp.zeros((16, 512), F32)
    for s, ref in enumerate((ga1, ga2, gav)):
        pick = ((row == 2 * s) & (lane == 0)) | ((row == 2 * s + 1) & (lane == 1))
        edges += dot_nt(pick.astype(F32).astype(BF16), ref[:, 0:128].astype(BF16))
    edge_s[...] = edges.astype(BF16)
    edge_copy = neighbour(edge_s, edge_r, 1, previous)
    edge_copy.start()
    edge_copy.wait_recv()
    wrow[0:16, :] = edge_r[...].astype(F32) * (me < 15).astype(F32)
    hcol[...] = jnp.transpose(wrow[...])
    sal_s[...] = jnp.zeros((8, 512), F32)

    def adjoint(block):
        rows = pl.ds(pl.multiple_of(block * 32, 32), 32)
        weight = wcol[rows, :]
        halo = hcol[rows, :]
        total = jnp.zeros((32, 512), F32)
        for s, (grad, stream, out) in enumerate(((ga1, x1, o1), (ga2, x2, o2), (gav, xv, ov))):
            field = grad[rows, :]
            next_one, next_two = halo[:, 2 * s : 2 * s + 1], halo[:, 2 * s + 1 : 2 * s + 2]
            one = jnp.where(lane32 == 511, next_one, pltpu.roll(field, 511, 1))
            two = jnp.where(
                lane32 == 511, next_two, jnp.where(lane32 == 510, next_one, pltpu.roll(field, 510, 1)))
            full = (
                weight[:, 3 * s : 3 * s + 1] * field
                + weight[:, 3 * s + 1 : 3 * s + 2] * one
                + weight[:, 3 * s + 2 : 3 * s + 3] * two
            )
            out[rows, :] = full.astype(BF16)
            total += stream[rows, :].astype(F32) * full
        sal_s[...] += total[0:8] + total[8:16] + total[16:24] + total[24:32]

    loop(0, 16, adjoint)
    outs = [
        pltpu.make_async_copy(a, b, out_sem.at[n])
        for n, (a, b) in enumerate(((o1, o1_h), (o2, o2_h), (ov, ov_h), (osk, osk_h), (osal, osal_h)))
    ]
    for n in range(3):
        outs[n].start()

    def sal_copy(i, to, slot):
        return pltpu.make_async_remote_copy(
            src_ref=sal_s, dst_ref=sal_r.at[slot], send_sem=sal_send.at[i], recv_sem=sal_recv.at[i],
            device_id=(me, to), device_id_type=MESH)

    loop(1, 8, lambda i: sal_copy(i, lax.rem(chan + i, 8), chan).start())
    sal_r[chan] = sal_s[...]

    own(6, slot_of(part_s), rs_r).wait()
    wait_arrived(6, slot_of(part_s), rs_r)
    for side in range(2):
        total = rs_r[side].astype(F32)
        for chip in range(1, 8):
            total += rs_r[2 * chip + side].astype(F32)
        osk[:, side * 256 : side * 256 + 256] = total
    outs[3].start()

    def sal_arrived(i):
        origin = lax.rem(chan + 8 - i, 8)
        sal_copy(i, origin, origin).wait_recv()

    loop(1, 8, sal_arrived)
    total = sal_r[0]
    for n in range(1, 8):
        total += sal_r[n]
    total = jnp.sum(total, axis=0, keepdims=True) * (3.0 * D) ** (-0.5)
    total = jnp.broadcast_to(total, (8, 512))
    osal[...] = pltpu.roll(total, 512 - chan * 64, 1)[:, 0:128]
    outs[4].start()

    tail_copy.wait_send()
    edge_copy.wait_send()
    swap.wait_send()
    wait_sent(0, block_of(taps_h), taps_r)
    wait_sent(1, block_of(gg_s), gg_r)
    wait_sent(2, block_of(g_s), g_r)

    def filter_sent(chip):
        @pl.when(2 * chip + half != me)
        def _():
            filter_copy(chip).wait_send()

    loop(0, 8, filter_sent)
    wait_sent(4, slot_of(mix_s), mix_r)
    wait_sent(5, slot_of(gmix_s), gmix_r)
    wait_sent(6, slot_of(part_s), rs_r)
    loop(1, 8, lambda i: sal_copy(i, lax.rem(chan + i, 8), chan).wait_send())
    for out in outs:
        out.wait()


def on_device(*arrays):
    one, two, value, grad, taps, short, gain, sketch = arrays
    tables = [jnp.asarray(t) for t in host_tables()]
    operands = [one, two, value, grad, taps, short, gain.reshape(1, 512), sketch] + tables

    def vmem(shape, dtype=BF16):
        return pltpu.VMEM(shape, dtype)

    square = (512, 512)
    parts = (16, 32, 512)
    scratch = [
        *[vmem(square) for _ in range(4)], vmem((3, 3, 512), F32), vmem((1, 512), F32), vmem((2, 1024, 512)),
        *[vmem(t.shape, t.dtype) for t in tables],
        vmem((128, 512), F32), vmem((512, 128), F32),
        vmem((16, 512)), vmem((16, 512)), vmem((16, 512)), vmem((16, 512)), vmem((512, 128), F32),
        vmem(square), vmem(square), vmem(square, F32), vmem(square, F32),
        *[vmem(parts) for _ in range(3)],
        vmem((4, 512, 256), F32), vmem((ROWS, 256)), vmem((ROWS, 256)),
        *[vmem((ROWS, 256), F32) for _ in range(4)], vmem((4, 512, 256)), vmem((4, 512, 256)),
        *[vmem(parts) for _ in range(3)], vmem((8, 2, 32, 512)), vmem(parts), vmem(parts),
        vmem((16, 64, 256)), vmem((16, 64, 256)),
        *[vmem(square, F32) for _ in range(3)], vmem((8, 512), F32), vmem((8, 8, 512), F32),
        *[vmem(square) for _ in range(3)], vmem((8, 128), F32), vmem((64, 512), F32),
        pltpu.SemaphoreType.DMA((17,)), pltpu.SemaphoreType.DMA((7,)), pltpu.SemaphoreType.DMA((5,)),
        pltpu.SemaphoreType.DMA((7, 16)), pltpu.SemaphoreType.DMA((7, 16)),
        pltpu.SemaphoreType.DMA((3,)), pltpu.SemaphoreType.DMA((3,)),
        pltpu.SemaphoreType.DMA((8,)), pltpu.SemaphoreType.DMA((8,)),
    ]
    grad_one, grad_two, grad_value, saliency, sketched = pl.pallas_call(
        kernel,
        out_shape=[
            *[jax.ShapeDtypeStruct(square, BF16) for _ in range(3)],
            jax.ShapeDtypeStruct((8, 128), F32),
            jax.ShapeDtypeStruct((64, 512), F32),
        ],
        in_specs=[pl.BlockSpec(memory_space=pl.ANY) for _ in operands],
        out_specs=[pl.BlockSpec(memory_space=pl.ANY) for _ in range(5)],
        scratch_shapes=scratch,
        compiler_params=pltpu.CompilerParams(
            collective_id=0, has_side_effects=True, vmem_limit_bytes=56 * 1024 * 1024),
    )(*operands)
    return grad_one, grad_two, grad_value, saliency[0, :64], sketched


def solution(mesh):
    return jax.shard_map(
        on_device,
        mesh=mesh,
        in_specs=(
            P("chan", "seq"),
            P("chan", "seq"),
            P("chan", "seq"),
            P("chan", "seq"),
            P("chan", "seq"),
            P(None, None, "chan"),
            P("chan"),
            P(None, "seq"),
        ),
        out_specs=(
            P("chan", "seq"),
            P("chan", "seq"),
            P("chan", "seq"),
            P(("seq", "chan")),
            P("seq", "chan"),
        ),
        check_vma=False,
    )
```

```python
import functools
import math

import jax
import jax.numpy as jnp
import numpy as np
from jax import lax
from jax.experimental import pallas as pl
from jax.experimental.pallas import tpu as pltpu
from jax.sharding import PartitionSpec as P

D = 4096
MESH = pl.DeviceIdType.MESH
F32 = jnp.float32
BF16 = jnp.bfloat16
ROOT = math.sqrt(0.5)
FREQS = [k1 + 32 * q for k1 in range(1, 16) for q in range(4)] + [0, 32, 64, 16, 48]
ROWS = 32 * len(FREQS)


def split_host(table):
    high = table.astype(jnp.bfloat16)
    low = (table - high.astype(np.float64)).astype(jnp.bfloat16)
    return high, low


def host_tables():
    shard = np.arange(16)
    k1 = np.arange(16)
    first = np.zeros((4, 32, 16))
    for tile in range(4):
        angle = 2 * np.pi * np.outer(k1, 4 * shard + tile) / 128
        first[tile, :16] = np.cos(angle)
        first[tile, 16:] = -np.sin(angle)
        first[tile, 16] = (-1.0) ** shard
    eye = np.eye(16)
    wide = np.einsum("tks,cd->tkcsd", first, eye).reshape(4, 512, 256)
    back = np.einsum("tks,cd->tsckd", first, eye).reshape(4, 256, 512) * (2.0 / 16384)
    lane = np.arange(128)
    angle = 2 * np.pi * np.outer(lane, lane) / 128
    cos, sin = np.cos(angle), np.sin(angle)
    inner = np.block([[cos, -sin], [sin, cos]])
    inner_back = np.block([[cos, sin], [-sin, cos]])
    twist = 2 * np.pi * np.outer(np.array(FREQS + [0] * 7), lane) / 16384
    twist = np.concatenate([twist, twist], axis=1)
    return (
        *split_host(wide),
        *split_host(back),
        *split_host(inner),
        *split_host(inner_back),
        np.cos(twist).astype(np.float32),
        np.sin(twist).astype(np.float32),
    )


def dot(left, right):
    return jnp.dot(left, right, preferred_element_type=F32)


def dot_nt(left, right):
    return lax.dot_general(left, right, (((1,), (1,)), ((), ())), preferred_element_type=F32)


def halves(value):
    high = value.astype(BF16)
    return high, (value - high.astype(F32)).astype(BF16)


def loop(first, last, body):
    def step(index, carry):
        body(index)
        return carry

    lax.fori_loop(first, last, step, 0)


def kernel(
    x1_h, x2_h, xv_h, go_h, taps_h, short_h, gain_h, sk_h,
    c1h_h, c1l_h, dh_h, dl_h, mh_h, ml_h, nh_h, nl_h, twc_h, tws_h,
    o1_h, o2_h, ov_h, osal_h, osk_h,
    x1, x2, xv, go, short, gain, sk,
    c1h, c1l, dh, dl, mh, ml, nh, nl, twc, tws,
    wrow, wcol, tail_s, tail_r, edge_s, edge_r, hcol,
    act2, actv,
    pair_s, pair_r, taps_r,
    y, zh, zl, spec_t, spec_p, e, wh, wl,
    gf_s, gf_r, mm_s, mm_r,
    part_s, rs_r, ga1, ga2, gav, sal_s, sal_r, o1, o2, ov, osal, osk,
    load_sem, out_sem, send_sem, recv_sem, halo_send, halo_recv, sal_send, sal_recv,
):
    me = lax.axis_index("seq")
    chan = lax.axis_index("chan")
    core = lax.rem(me, 2)
    half = me // 8
    sibling = me + 1 - 2 * core
    following = lax.rem(me + 1, 16)
    previous = lax.rem(me + 15, 16)

    loads = [
        (x1_h, x1), (x2_h, x2), (xv_h, xv), (go_h, go), (short_h, short), (gain_h, gain),
        (c1h_h, c1h), (c1l_h, c1l), (mh_h, mh), (ml_h, ml), (twc_h, twc), (tws_h, tws),
        (nh_h, nh), (nl_h, nl), (dh_h, dh), (dl_h, dl), (sk_h, sk.at[core]),
    ]
    loads = [pltpu.make_async_copy(a, b, load_sem.at[n]) for n, (a, b) in enumerate(loads)]
    for load in loads:
        load.start()

    barrier = pltpu.get_barrier_semaphore()
    loop(1, 16, lambda i: pl.semaphore_signal(
        barrier, inc=1, device_id=(lax.rem(me + i, 16), chan), device_id_type=MESH))
    loop(1, 8, lambda i: pl.semaphore_signal(
        barrier, inc=1, device_id=(me, lax.rem(chan + i, 8)), device_id_type=MESH))

    def block_of(ref):
        return lambda to: ref.at[pl.ds(pl.multiple_of(to * 32, 32), 32)]

    def slot_of(ref):
        return lambda to: ref.at[to]

    def send_all(kind, source, target):
        def one(i):
            to = lax.rem(me + i, 16)
            pltpu.make_async_remote_copy(
                src_ref=source(to), dst_ref=target.at[me],
                send_sem=send_sem.at[kind], recv_sem=recv_sem.at[kind],
                device_id=(to, chan), device_id_type=MESH,
            ).start()

        loop(1, 16, one)
        pltpu.make_async_copy(source(me), target.at[me], recv_sem.at[kind]).start()

    def wait_bytes(ref, sem):
        pltpu.make_async_copy(ref, ref, sem).wait()

    def neighbour(source, target, n, to):
        return pltpu.make_async_remote_copy(
            src_ref=source, dst_ref=target, send_sem=halo_send.at[n], recv_sem=halo_recv.at[n],
            device_id=(to, chan), device_id_type=MESH)

    for n in range(6):
        loads[n].wait()
    row = lax.broadcasted_iota(jnp.int32, (16, 128), 0)
    lane = lax.broadcasted_iota(jnp.int32, (16, 128), 1)
    tails = jnp.zeros((16, 512), F32)
    for s, ref in enumerate((x1, x2, xv)):
        pick = ((row == 2 * s) & (lane == 126)) | ((row == 2 * s + 1) & (lane == 127))
        tails += dot_nt(pick.astype(F32).astype(BF16), ref[:, 384:512])
    tail_s[...] = tails.astype(BF16)

    pl.semaphore_wait(barrier, 22)
    tail_copy = neighbour(tail_s, tail_r, 0, following)
    tail_copy.start()
    send_all(0, block_of(taps_h), taps_r)

    wrow[...] = jnp.zeros((128, 512), F32)
    for s in range(3):
        wrow[3 * s : 3 * s + 3, :] = short[s]
    wrow[9:10, :] = gain[...]
    wcol[...] = jnp.transpose(wrow[...])

    tail_copy.wait_recv()
    wrow[0:16, :] = tail_r[...].astype(F32) * (me > 0).astype(F32)
    hcol[...] = jnp.transpose(wrow[...])

    lane16 = lax.broadcasted_iota(jnp.int32, (16, 512), 1)

    def rows_of(block, h):
        return pl.ds(pl.multiple_of(block * 32 + h * 16, 16), 16)

    def gate(h):
        def body(block):
            rows = rows_of(block, h)
            weight = wcol[rows, :]
            halo = hcol[rows, :]

            def short_filter(ref, s):
                field = ref[rows, :].astype(F32)
                before, last = halo[:, 2 * s : 2 * s + 1], halo[:, 2 * s + 1 : 2 * s + 2]
                one = jnp.where(lane16 == 0, last, pltpu.roll(field, 1, 1))
                two = jnp.where(lane16 == 0, before, jnp.where(lane16 == 1, last, pltpu.roll(field, 2, 1)))
                return (
                    weight[:, 3 * s : 3 * s + 1] * field
                    + weight[:, 3 * s + 1 : 3 * s + 2] * one
                    + weight[:, 3 * s + 2 : 3 * s + 3] * two
                )

            first = short_filter(x1, 0)
            pair_s[h, block, 0] = (go[rows, :].astype(F32) * first).astype(BF16)
            second = short_filter(x2, 1)
            value = short_filter(xv, 2)
            act2[rows, :] = second
            actv[rows, :] = value
            pair_s[h, block, 1] = (second * value).astype(BF16)

        loop(0, 16, body)

    for h in range(2):
        gate(h)
        send_all(1 + h, slot_of(pair_s.at[h]), pair_r.at[h])
    swap = neighbour(sk_h, sk.at[core], 2, sibling)
    swap.start()

    def first_rows(tile, part, k1):
        return y[tile, pl.ds(pl.multiple_of(part * 256 + k1 * 16, 16), 16), :]

    def store_z(index, re, im):
        for g in range(2):
            rows = pl.ds(pl.multiple_of(index * 32 + g * 16, 16), 16)
            side = slice(g * 128, g * 128 + 128)
            high, low = halves(jnp.concatenate([re[:, side], im[:, side]], axis=1))
            zh[rows, :] = high
            zl[rows, :] = low

    def twist(index, re, im):
        cos, sin = twc[pl.ds(index, 1), :], tws[pl.ds(index, 1), :]
        store_z(index, re * cos + im * sin, im * cos - re * sin)

    def forward(source, spec):
        def stage(tile):
            lanes = pl.ds(pl.multiple_of(tile * 128, 128), 128)
            right = jnp.concatenate([source(g, lanes).reshape(256, 128) for g in range(2)], axis=1)
            y[tile] = dot(c1h[tile], right) + dot(c1l[tile], right)

        loop(0, 4, stage)

        def butterfly(k1):
            r0, r1, r2, r3 = [first_rows(t, 0, k1) for t in range(4)]
            i0, i1, i2, i3 = [first_rows(t, 1, k1) for t in range(4)]
            ar, ai, br, bi = r0 + r2, i0 + i2, r0 - r2, i0 - i2
            cr, ci, dr, di = r1 + r3, i1 + i3, r1 - r3, i1 - i3
            base = (k1 - 1) * 4
            twist(base, ar + cr, ai + ci)
            twist(base + 1, br + di, bi - dr)
            twist(base + 2, ar - cr, ai - ci)
            twist(base + 3, br - di, bi + dr)

        loop(1, 16, butterfly)
        r0, r1, r2, r3 = [first_rows(t, 0, 0) for t in range(4)]
        none = jnp.zeros_like(r0)
        store_z(60, r0 + r1 + r2 + r3, none)
        twist(61, r0 - r2, r3 - r1)
        twist(62, r0 - r1 + r2 - r3, none)
        r0, r1, r2, r3 = [first_rows(t, 1, 0) for t in range(4)]
        twist(63, r0 + ROOT * (r1 - r3), -r2 - ROOT * (r1 + r3))
        twist(64, r0 - ROOT * (r1 - r3), r2 - ROOT * (r1 + r3))

        def last(chunk):
            rows = pl.ds(pl.multiple_of(chunk * 416, 16), 416)
            out = dot(zh[rows, :], mh[...]) + dot(zl[rows, :], mh[...]) + dot(zh[rows, :], ml[...])
            spec[pl.ds(chunk * 13, 13)] = out.reshape(13, 32, 256)

        loop(0, 5, last)

    def times(left, right, sign):
        lr, li = left[..., 0:128], left[..., 128:256] * sign
        rr, ri = right[..., 0:128], right[..., 128:256]
        return jnp.concatenate([lr * rr - li * ri, lr * ri + li * rr], axis=2)

    def inverse(product, count, store):
        size = 16 * count
        wide = 128 * count

        def first(chunk):
            high, low = halves(product(pl.ds(chunk * 13, 13)).reshape(13 * size, 256))
            rows = pl.ds(pl.multiple_of(chunk * 13 * size, 16), 13 * size)
            e[rows, :] = dot(high, nh[...]) + dot(low, nh[...]) + dot(high, nl[...])

        loop(0, 5, first)

        def untwist(index):
            cos, sin = twc[pl.ds(index, 1), :][:, 0:wide], tws[pl.ds(index, 1), :][:, 0:wide]
            parts = [e[pl.ds(pl.multiple_of(index * size + 16 * g, 16), 16), :] for g in range(count)]
            re = jnp.concatenate([p[:, 0:128] for p in parts], axis=1)
            im = jnp.concatenate([p[:, 128:256] for p in parts], axis=1)
            return re * cos - im * sin, im * cos + re * sin

        def store_w(tile, part, k1, value):
            rows = pl.ds(pl.multiple_of(part * 256 + k1 * 16, 16), 16)
            high, low = halves(value)
            wh[tile, rows, 0:wide] = high
            wl[tile, rows, 0:wide] = low

        def butterfly(k1):
            base = (k1 - 1) * 4
            (r0, i0), (r1, i1), (r2, i2), (r3, i3) = [untwist(base + q) for q in range(4)]
            ar, ai, br, bi = r0 + r2, i0 + i2, r0 - r2, i0 - i2
            cr, ci, dr, di = r1 + r3, i1 + i3, r1 - r3, i1 - i3
            store_w(0, 0, k1, ar + cr)
            store_w(0, 1, k1, ai + ci)
            store_w(1, 0, k1, br - di)
            store_w(1, 1, k1, bi + dr)
            store_w(2, 0, k1, ar - cr)
            store_w(2, 1, k1, ai - ci)
            store_w(3, 0, k1, br + di)
            store_w(3, 1, k1, bi - dr)

        loop(1, 16, butterfly)
        (r0, _), (r32, i32), (r64, _), (r16, i16), (r48, i48) = [untwist(60 + n) for n in range(5)]
        plus, minus = 0.5 * (r0 + r64), 0.5 * (r0 - r64)
        store_w(0, 0, 0, plus + r32)
        store_w(1, 0, 0, minus - i32)
        store_w(2, 0, 0, plus - r32)
        store_w(3, 0, 0, minus + i32)
        store_w(0, 1, 0, r16 + r48)
        store_w(1, 1, 0, ROOT * (r16 - i16 - r48 - i48))
        store_w(2, 1, 0, i48 - i16)
        store_w(3, 1, 0, ROOT * (r48 - i48 - r16 - i16))

        def last(tile):
            lanes = pl.ds(pl.multiple_of(tile * 128, 128), 128)
            high, low = wh[tile, :, 0:wide], wl[tile, :, 0:wide]
            out = (dot(dh[tile], high) + dot(dh[tile], low) + dot(dl[tile], high)).astype(BF16)
            for g in range(count):
                store(g, lanes, out[:, g * 128 : g * 128 + 128].reshape(16, 16, 128))

        loop(0, 4, last)

    def filter_copy(h, chip):
        return pltpu.make_async_remote_copy(
            src_ref=gf_s.at[h, pl.ds(2 * chip, 2)], dst_ref=gf_r.at[me - 8 * half, h],
            send_sem=send_sem.at[3 + h], recv_sem=recv_sem.at[3 + h],
            device_id=(2 * chip + half, chan), device_id_type=MESH)

    def filter_out(h):
        def product(index):
            return times(spec_p[h, index, 16:32, :], spec_p[h, index, 0:16, :], -1.0)

        def store(g, lanes, value):
            gf_s[h, :, :, lanes] = value

        inverse(product, 1, store)

        def one(n):
            chip = lax.rem(me // 2 + n, 8)

            @pl.when(2 * chip + half != me)
            def _():
                filter_copy(h, chip).start()

        loop(0, 8, one)

        @pl.when(core == half)
        def _():
            pltpu.make_async_copy(
                gf_s.at[h, pl.ds(2 * (me // 2), 2)], gf_r.at[me - 8 * half, h], recv_sem.at[3 + h]).start()

    def mixes_out(h):
        def product(index):
            taps = spec_t[index, h * 16 : h * 16 + 16, :]
            return jnp.concatenate(
                [times(taps, spec_p[h, index, 16:32, :], 1.0), times(taps, spec_p[h, index, 0:16, :], -1.0)],
                axis=1)

        def store(g, lanes, value):
            mm_s[h, :, g, :, lanes] = value

        inverse(product, 2, store)
        send_all(5 + h, slot_of(mm_s.at[h]), mm_r.at[h])

    for n in range(6, 16):
        loads[n].wait()
    wait_bytes(taps_r, recv_sem.at[0])
    forward(lambda g, lanes: taps_r[:, g * 16 : g * 16 + 16, lanes], spec_t)
    for h in range(2):
        wait_bytes(pair_r.at[h], recv_sem.at[1 + h])
        forward(lambda g, lanes: pair_r[h, :, g, :, lanes], spec_p.at[h])
        filter_out(h)
        mixes_out(h)

    def activations(h):
        wait_bytes(mm_r.at[h], recv_sem.at[5 + h])

        def body(block):
            rows = rows_of(block, h)
            skip = wcol[rows, 9:10]
            mixed = mm_r[h, block, 0].astype(F32) + skip * pair_s[h, block, 1].astype(F32)
            ga1[rows, :] = go[rows, :].astype(F32) * mixed
            grad_mix = mm_r[h, block, 1].astype(F32) + skip * pair_s[h, block, 0].astype(F32)
            ga2[rows, :] = grad_mix * actv[rows, :]
            gav[rows, :] = grad_mix * act2[rows, :]

        loop(0, 16, body)

    loads[16].wait()
    swap_in = neighbour(sk_h, sk.at[1 - core], 2, sibling)
    swap_in.wait_recv()
    for h in range(2):
        wait_bytes(gf_s.at[h], recv_sem.at[3 + h])

    def sketch_rows(block):
        rows = pl.ds(pl.multiple_of(block * 256, 256), 256)
        total = dot_nt(sk[0, rows, :], gf_r[:, :, 0].reshape(256, 512))
        total += dot_nt(sk[1, rows, :], gf_r[:, :, 1].reshape(256, 512))
        part_s[pl.ds(block * 4, 4)] = total.astype(BF16).reshape(4, 64, 256)

    loop(0, 4, sketch_rows)
    send_all(7, slot_of(part_s), rs_r)

    activations(0)
    activations(1)
    edges = jnp.zeros((16, 512), F32)
    for s, ref in enumerate((ga1, ga2, gav)):
        pick = ((row == 2 * s) & (lane == 0)) | ((row == 2 * s + 1) & (lane == 1))
        edges += dot_nt(pick.astype(F32).astype(BF16), ref[:, 0:128].astype(BF16))
    edge_s[...] = edges.astype(BF16)
    edge_copy = neighbour(edge_s, edge_r, 1, previous)
    edge_copy.start()
    edge_copy.wait_recv()
    wrow[0:16, :] = edge_r[...].astype(F32) * (me < 15).astype(F32)
    hcol[...] = jnp.transpose(wrow[...])
    sal_s[...] = jnp.zeros((8, 512), F32)

    def adjoint(block):
        rows = pl.ds(pl.multiple_of(block * 16, 16), 16)
        weight = wcol[rows, :]
        halo = hcol[rows, :]
        total = jnp.zeros((16, 512), F32)
        for s, (grad, stream, out) in enumerate(((ga1, x1, o1), (ga2, x2, o2), (gav, xv, ov))):
            field = grad[rows, :]
            next_one, next_two = halo[:, 2 * s : 2 * s + 1], halo[:, 2 * s + 1 : 2 * s + 2]
            one = jnp.where(lane16 == 511, next_one, pltpu.roll(field, 511, 1))
            two = jnp.where(
                lane16 == 511, next_two, jnp.where(lane16 == 510, next_one, pltpu.roll(field, 510, 1)))
            full = (
                weight[:, 3 * s : 3 * s + 1] * field
                + weight[:, 3 * s + 1 : 3 * s + 2] * one
                + weight[:, 3 * s + 2 : 3 * s + 3] * two
            )
            out[rows, :] = full.astype(BF16)
            total += stream[rows, :].astype(F32) * full
        sal_s[...] += total[0:8] + total[8:16]

    loop(0, 32, adjoint)
    outs = [
        pltpu.make_async_copy(a, b, out_sem.at[n])
        for n, (a, b) in enumerate(((o1, o1_h), (o2, o2_h), (ov, ov_h), (osk, osk_h), (osal, osal_h)))
    ]
    for n in range(3):
        outs[n].start()

    def sal_send_to(i):
        pltpu.make_async_remote_copy(
            src_ref=sal_s, dst_ref=sal_r.at[chan], send_sem=sal_send.at[0], recv_sem=sal_recv.at[0],
            device_id=(me, lax.rem(chan + i, 8)), device_id_type=MESH).start()

    loop(1, 8, sal_send_to)
    pltpu.make_async_copy(sal_s, sal_r.at[chan], sal_recv.at[0]).start()

    wait_bytes(rs_r, recv_sem.at[7])
    for side in range(2):
        total = rs_r[side].astype(F32)
        for chip in range(1, 8):
            total += rs_r[2 * chip + side].astype(F32)
        osk[:, side * 256 : side * 256 + 256] = total
    outs[3].start()

    wait_bytes(sal_r, sal_recv.at[0])
    total = sal_r[0]
    for n in range(1, 8):
        total += sal_r[n]
    total = jnp.sum(total, axis=0, keepdims=True) * (3.0 * D) ** (-0.5)
    total = jnp.broadcast_to(total, (8, 512))
    osal[...] = pltpu.roll(total, 512 - chan * 64, 1)[:, 0:128]
    outs[4].start()

    tail_copy.wait_send()
    edge_copy.wait_send()
    swap.wait_send()
    wait_bytes(taps_r.at[pl.ds(0, 15)], send_sem.at[0])
    for h in range(2):
        wait_bytes(pair_s.at[h, pl.ds(0, 15)], send_sem.at[1 + h])
        wait_bytes(mm_s.at[h, pl.ds(0, 15)], send_sem.at[5 + h])
        wait_bytes(gf_s.at[h, pl.ds(0, 14)], send_sem.at[3 + h])

        @pl.when(core != half)
        def _():
            wait_bytes(gf_s.at[h, pl.ds(14, 2)], send_sem.at[3 + h])

    wait_bytes(part_s.at[pl.ds(0, 15)], send_sem.at[7])
    wait_bytes(sal_r.at[pl.ds(0, 7)], sal_send.at[0])
    for out in outs:
        out.wait()


def on_device(*arrays):
    one, two, value, grad, taps, short, gain, sketch = arrays
    tables = [jnp.asarray(t) for t in host_tables()]
    operands = [one, two, value, grad, taps, short, gain.reshape(1, 512), sketch] + tables

    def vmem(shape, dtype=BF16):
        return pltpu.VMEM(shape, dtype)

    square = (512, 512)
    parts = (2, 16, 2, 16, 512)
    scratch = [
        *[vmem(square) for _ in range(4)], vmem((3, 3, 512), F32), vmem((1, 512), F32), vmem((2, 1024, 512)),
        *[vmem(t.shape, t.dtype) for t in tables],
        vmem((128, 512), F32), vmem((512, 128), F32),
        vmem((16, 512)), vmem((16, 512)), vmem((16, 512)), vmem((16, 512)), vmem((512, 128), F32),
        vmem(square, F32), vmem(square, F32),
        vmem(parts), vmem(parts), vmem((16, 32, 512)),
        vmem((4, 512, 256), F32), vmem((ROWS, 256)), vmem((ROWS, 256)),
        vmem((65, 32, 256), F32), vmem((2, 65, 32, 256), F32), vmem((ROWS, 256), F32),
        vmem((4, 512, 256)), vmem((4, 512, 256)),
        vmem((2, 16, 16, 512)), vmem((8, 2, 2, 16, 512)), vmem(parts), vmem(parts),
        vmem((16, 64, 256)), vmem((16, 64, 256)),
        *[vmem(square, F32) for _ in range(3)], vmem((8, 512), F32), vmem((8, 8, 512), F32),
        *[vmem(square) for _ in range(3)], vmem((8, 128), F32), vmem((64, 512), F32),
        pltpu.SemaphoreType.DMA((17,)), pltpu.SemaphoreType.DMA((5,)),
        pltpu.SemaphoreType.DMA((8,)), pltpu.SemaphoreType.DMA((8,)),
        pltpu.SemaphoreType.DMA((3,)), pltpu.SemaphoreType.DMA((3,)),
        pltpu.SemaphoreType.DMA((1,)), pltpu.SemaphoreType.DMA((1,)),
    ]
    grad_one, grad_two, grad_value, saliency, sketched = pl.pallas_call(
        kernel,
        out_shape=[
            *[jax.ShapeDtypeStruct(square, BF16) for _ in range(3)],
            jax.ShapeDtypeStruct((8, 128), F32),
            jax.ShapeDtypeStruct((64, 512), F32),
        ],
        in_specs=[pl.BlockSpec(memory_space=pl.ANY) for _ in operands],
        out_specs=[pl.BlockSpec(memory_space=pl.ANY) for _ in range(5)],
        scratch_shapes=scratch,
        compiler_params=pltpu.CompilerParams(
            collective_id=0, has_side_effects=True, vmem_limit_bytes=56 * 1024 * 1024),
    )(*operands)
    return grad_one, grad_two, grad_value, saliency[0, :64], sketched


def solution(mesh):
    return jax.shard_map(
        on_device,
        mesh=mesh,
        in_specs=(
            P("chan", "seq"),
            P("chan", "seq"),
            P("chan", "seq"),
            P("chan", "seq"),
            P("chan", "seq"),
            P(None, None, "chan"),
            P("chan"),
            P(None, "seq"),
        ),
        out_specs=(
            P("chan", "seq"),
            P("chan", "seq"),
            P("chan", "seq"),
            P(("seq", "chan")),
            P("seq", "chan"),
        ),
        check_vma=False,
    )
```

```python
import functools
import math

import jax
import jax.numpy as jnp
import numpy as np
from jax import lax
from jax.experimental import pallas as pl
from jax.experimental.pallas import tpu as pltpu
from jax.sharding import PartitionSpec as P

D = 4096
MESH = pl.DeviceIdType.MESH
F32 = jnp.float32
BF16 = jnp.bfloat16
ROOT = math.sqrt(0.5)
FREQS = [k1 + 32 * q for k1 in range(1, 16) for q in range(4)] + [0, 32, 64, 16, 48]
ROWS = 32 * len(FREQS)


def split_host(table):
    high = table.astype(jnp.bfloat16)
    low = (table - high.astype(np.float64)).astype(jnp.bfloat16)
    return high, low


def host_tables():
    shard = np.arange(16)
    k1 = np.arange(16)
    first = np.zeros((4, 32, 16))
    for tile in range(4):
        angle = 2 * np.pi * np.outer(k1, 4 * shard + tile) / 128
        first[tile, :16] = np.cos(angle)
        first[tile, 16:] = -np.sin(angle)
        first[tile, 16] = (-1.0) ** shard
    eye = np.eye(16)
    wide = np.einsum("tks,cd->tkcsd", first, eye).reshape(4, 512, 256)
    back = np.einsum("tks,cd->tsckd", first, eye).reshape(4, 256, 512) * (2.0 / 16384)
    lane = np.arange(128)
    angle = 2 * np.pi * np.outer(lane, lane) / 128
    cos, sin = np.cos(angle), np.sin(angle)
    inner = np.block([[cos, -sin], [sin, cos]])
    inner_back = np.block([[cos, sin], [-sin, cos]])
    twist = 2 * np.pi * np.outer(np.array(FREQS + [0] * 7), lane) / 16384
    twist = np.concatenate([twist, twist], axis=1)
    return (
        *split_host(wide),
        *split_host(back),
        *split_host(inner),
        *split_host(inner_back),
        np.cos(twist).astype(np.float32),
        np.sin(twist).astype(np.float32),
    )


def dot(left, right):
    return jnp.dot(left, right, preferred_element_type=F32)


def dot_nt(left, right):
    return lax.dot_general(left, right, (((1,), (1,)), ((), ())), preferred_element_type=F32)


def halves(value):
    high = value.astype(BF16)
    return high, (value - high.astype(F32)).astype(BF16)


def multiple(value, of):
    return value if isinstance(value, int) else pl.multiple_of(value, of)


def unrolled(first, last, body):
    for index in range(first, last):
        body(index)


def loop(first, last, body):
    def step(index, carry):
        body(index)
        return carry

    lax.fori_loop(first, last, step, 0)


def kernel(
    x1_h, x2_h, xv_h, go_h, taps_h, short_h, gain_h, sk_h,
    c1h_h, c1l_h, dh_h, dl_h, mh_h, ml_h, nh_h, nl_h, twc_h, tws_h,
    o1_h, o2_h, ov_h, osal_h, osk_h,
    x1, x2, xv, go, short, gain, sk,
    c1h, c1l, dh, dl, mh, ml, nh, nl, twc, tws,
    wrow, wcol, tail_s, tail_r, edge_s, edge_r, hcol,
    act2, actv,
    pair_s, pair_r, taps_r,
    y, zh, zl, spec_t, spec_p, e, wh, wl,
    gf_s, gf_r, mm_s, mm_r,
    part_s, rs_r, first_tile, sal_s, sal_r, o1, o2, ov, osal, osk,
    load_sem, out_sem, send_sem, recv_sem, halo_send, halo_recv, sal_send, sal_recv,
):
    me = lax.axis_index("seq")
    chan = lax.axis_index("chan")
    core = lax.rem(me, 2)
    half = me // 8
    sibling = me + 1 - 2 * core
    following = lax.rem(me + 1, 16)
    previous = lax.rem(me + 15, 16)

    loads = [
        (x1_h, x1), (x2_h, x2), (xv_h, xv), (go_h, go), (short_h, short), (gain_h, gain),
        (c1h_h, c1h), (c1l_h, c1l), (mh_h, mh), (ml_h, ml), (twc_h, twc), (tws_h, tws),
        (nh_h, nh), (nl_h, nl), (dh_h, dh), (dl_h, dl), (sk_h, sk.at[core]),
    ]
    loads = [pltpu.make_async_copy(a, b, load_sem.at[n]) for n, (a, b) in enumerate(loads)]
    for load in loads:
        load.start()

    barrier = pltpu.get_barrier_semaphore()
    loop(1, 16, lambda i: pl.semaphore_signal(
        barrier, inc=1, device_id=(lax.rem(me + i, 16), chan), device_id_type=MESH))
    loop(1, 8, lambda i: pl.semaphore_signal(
        barrier, inc=1, device_id=(me, lax.rem(chan + i, 8)), device_id_type=MESH))

    def block_of(ref):
        return lambda to: ref.at[pl.ds(multiple(to * 32, 32), 32)]

    def slot_of(ref):
        return lambda to: ref.at[to]

    def send_all(kind, source, target, begin=1, end=16):
        def one(i):
            to = lax.rem(me + i, 16)
            pltpu.make_async_remote_copy(
                src_ref=source(to), dst_ref=target.at[me],
                send_sem=send_sem.at[kind], recv_sem=recv_sem.at[kind],
                device_id=(to, chan), device_id_type=MESH,
            ).start()

        loop(begin, end, one)
        if end == 16:
            pltpu.make_async_copy(source(me), target.at[me], recv_sem.at[kind]).start()

    def wait_bytes(ref, sem):
        pltpu.make_async_copy(ref, ref, sem).wait()

    def neighbour(source, target, n, to):
        return pltpu.make_async_remote_copy(
            src_ref=source, dst_ref=target, send_sem=halo_send.at[n], recv_sem=halo_recv.at[n],
            device_id=(to, chan), device_id_type=MESH)

    pl.semaphore_wait(barrier, 22)
    send_all(0, block_of(taps_h), taps_r, 1, 7)

    for n in range(3):
        loads[n].wait()
    row = lax.broadcasted_iota(jnp.int32, (16, 128), 0)
    lane = lax.broadcasted_iota(jnp.int32, (16, 128), 1)
    tails = jnp.zeros((16, 512), F32)
    for s, ref in enumerate((x1, x2, xv)):
        pick = ((row == 2 * s) & (lane == 126)) | ((row == 2 * s + 1) & (lane == 127))
        tails += dot_nt(pick.astype(F32).astype(BF16), ref[:, 384:512])
    tail_s[...] = tails.astype(BF16)
    tail_copy = neighbour(tail_s, tail_r, 0, following)
    tail_copy.start()
    send_all(0, block_of(taps_h), taps_r, 7, 16)
    for n in range(3, 6):
        loads[n].wait()

    wrow[...] = jnp.zeros((128, 512), F32)
    for s in range(3):
        wrow[3 * s : 3 * s + 3, :] = short[s]
    wrow[9:10, :] = gain[...]
    wcol[...] = jnp.transpose(wrow[...])

    tail_copy.wait_recv()
    wrow[0:16, :] = tail_r[...].astype(F32) * (me > 0).astype(F32)
    hcol[...] = jnp.transpose(wrow[...])

    lane16 = lax.broadcasted_iota(jnp.int32, (16, 512), 1)

    def rows_of(block, h):
        return pl.ds(multiple(block * 32 + h * 16, 16), 16)

    def gate(h):
        def body(block):
            rows = rows_of(block, h)
            weight = wcol[rows, :]
            halo = hcol[rows, :]

            def short_filter(ref, s):
                field = ref[rows, :].astype(F32)
                before, last = halo[:, 2 * s : 2 * s + 1], halo[:, 2 * s + 1 : 2 * s + 2]
                one = jnp.where(lane16 == 0, last, pltpu.roll(field, 1, 1))
                two = jnp.where(lane16 == 0, before, jnp.where(lane16 == 1, last, pltpu.roll(field, 2, 1)))
                return (
                    weight[:, 3 * s : 3 * s + 1] * field
                    + weight[:, 3 * s + 1 : 3 * s + 2] * one
                    + weight[:, 3 * s + 2 : 3 * s + 3] * two
                )

            first = short_filter(x1, 0)
            pair_s[h, block, 0] = (go[rows, :].astype(F32) * first).astype(BF16)
            second = short_filter(x2, 1)
            value = short_filter(xv, 2)
            act2[rows, :] = second
            actv[rows, :] = value
            pair_s[h, block, 1] = (second * value).astype(BF16)

        loop(0, 16, body)

    for h in range(2):
        gate(h)
        send_all(1 + h, slot_of(pair_s.at[h]), pair_r.at[h])
    swap = neighbour(sk_h, sk.at[core], 3, sibling)
    swap.start()

    def first_rows(tile, part, k1):
        return y[tile, pl.ds(multiple(part * 256 + k1 * 16, 16), 16), :]

    def store_z(index, re, im):
        for g in range(2):
            rows = pl.ds(multiple(index * 32 + g * 16, 16), 16)
            side = slice(g * 128, g * 128 + 128)
            high, low = halves(jnp.concatenate([re[:, side], im[:, side]], axis=1))
            zh[rows, :] = high
            zl[rows, :] = low

    def twist(index, re, im):
        cos, sin = twc[pl.ds(index, 1), :], tws[pl.ds(index, 1), :]
        store_z(index, re * cos + im * sin, im * cos - re * sin)

    def forward(source, spec):
        def stage(tile):
            lanes = pl.ds(multiple(tile * 128, 128), 128)
            right = jnp.concatenate([source(g, lanes).reshape(256, 128) for g in range(2)], axis=1)
            y[tile] = dot(c1h[tile], right) + dot(c1l[tile], right)

        unrolled(0, 4, stage)

        def butterfly(k1):
            r0, r1, r2, r3 = [first_rows(t, 0, k1) for t in range(4)]
            i0, i1, i2, i3 = [first_rows(t, 1, k1) for t in range(4)]
            ar, ai, br, bi = r0 + r2, i0 + i2, r0 - r2, i0 - i2
            cr, ci, dr, di = r1 + r3, i1 + i3, r1 - r3, i1 - i3
            base = (k1 - 1) * 4
            twist(base, ar + cr, ai + ci)
            twist(base + 1, br + di, bi - dr)
            twist(base + 2, ar - cr, ai - ci)
            twist(base + 3, br - di, bi + dr)

        unrolled(1, 16, butterfly)
        r0, r1, r2, r3 = [first_rows(t, 0, 0) for t in range(4)]
        none = jnp.zeros_like(r0)
        store_z(60, r0 + r1 + r2 + r3, none)
        twist(61, r0 - r2, r3 - r1)
        twist(62, r0 - r1 + r2 - r3, none)
        r0, r1, r2, r3 = [first_rows(t, 1, 0) for t in range(4)]
        twist(63, r0 + ROOT * (r1 - r3), -r2 - ROOT * (r1 + r3))
        twist(64, r0 - ROOT * (r1 - r3), r2 - ROOT * (r1 + r3))

        def last(chunk):
            rows = pl.ds(multiple(chunk * 416, 16), 416)
            out = dot(zh[rows, :], mh[...]) + dot(zl[rows, :], mh[...]) + dot(zh[rows, :], ml[...])
            spec[pl.ds(chunk * 13, 13)] = out.reshape(13, 32, 256)

        unrolled(0, 5, last)

    def times(left, right, sign):
        lr, li = left[..., 0:128], left[..., 128:256] * sign
        rr, ri = right[..., 0:128], right[..., 128:256]
        return jnp.concatenate([lr * rr - li * ri, lr * ri + li * rr], axis=2)

    def inverse(product, count, store):
        size = 16 * count
        wide = 128 * count

        def first(chunk):
            high, low = halves(product(pl.ds(chunk * 13, 13)).reshape(13 * size, 256))
            rows = pl.ds(multiple(chunk * 13 * size, 16), 13 * size)
            e[rows, :] = dot(high, nh[...]) + dot(low, nh[...]) + dot(high, nl[...])

        unrolled(0, 5, first)

        def untwist(index):
            cos, sin = twc[pl.ds(index, 1), :][:, 0:wide], tws[pl.ds(index, 1), :][:, 0:wide]
            parts = [e[pl.ds(multiple(index * size + 16 * g, 16), 16), :] for g in range(count)]
            re = jnp.concatenate([p[:, 0:128] for p in parts], axis=1)
            im = jnp.concatenate([p[:, 128:256] for p in parts], axis=1)
            return re * cos - im * sin, im * cos + re * sin

        def store_w(tile, part, k1, value):
            rows = pl.ds(multiple(part * 256 + k1 * 16, 16), 16)
            high, low = halves(value)
            wh[tile, rows, 0:wide] = high
            wl[tile, rows, 0:wide] = low

        def butterfly(k1):
            base = (k1 - 1) * 4
            (r0, i0), (r1, i1), (r2, i2), (r3, i3) = [untwist(base + q) for q in range(4)]
            ar, ai, br, bi = r0 + r2, i0 + i2, r0 - r2, i0 - i2
            cr, ci, dr, di = r1 + r3, i1 + i3, r1 - r3, i1 - i3
            store_w(0, 0, k1, ar + cr)
            store_w(0, 1, k1, ai + ci)
            store_w(1, 0, k1, br - di)
            store_w(1, 1, k1, bi + dr)
            store_w(2, 0, k1, ar - cr)
            store_w(2, 1, k1, ai - ci)
            store_w(3, 0, k1, br + di)
            store_w(3, 1, k1, bi - dr)

        unrolled(1, 16, butterfly)
        (r0, _), (r32, i32), (r64, _), (r16, i16), (r48, i48) = [untwist(60 + n) for n in range(5)]
        plus, minus = 0.5 * (r0 + r64), 0.5 * (r0 - r64)
        store_w(0, 0, 0, plus + r32)
        store_w(1, 0, 0, minus - i32)
        store_w(2, 0, 0, plus - r32)
        store_w(3, 0, 0, minus + i32)
        store_w(0, 1, 0, r16 + r48)
        store_w(1, 1, 0, ROOT * (r16 - i16 - r48 - i48))
        store_w(2, 1, 0, i48 - i16)
        store_w(3, 1, 0, ROOT * (r48 - i48 - r16 - i16))

        def last(tile):
            lanes = pl.ds(multiple(tile * 128, 128), 128)
            high, low = wh[tile, :, 0:wide], wl[tile, :, 0:wide]
            out = (dot(dh[tile], high) + dot(dh[tile], low) + dot(dl[tile], high)).astype(BF16)
            for g in range(count):
                store(g, lanes, out[:, g * 128 : g * 128 + 128].reshape(16, 16, 128))

        unrolled(0, 4, last)

    def filter_out():
        def product(index):
            return jnp.concatenate(
                [times(spec_p[h, index, 16:32, :], spec_p[h, index, 0:16, :], -1.0) for h in range(2)],
                axis=1)

        def store(g, lanes, value):
            gf_s[:, g * 16 : g * 16 + 16, lanes] = value

        inverse(product, 2, store)

        def one(n):
            chip = lax.rem(me // 2 + n, 8)

            @pl.when(2 * chip + half != me)
            def _():
                pltpu.make_async_remote_copy(
                    src_ref=gf_s.at[pl.ds(2 * chip, 2)], dst_ref=gf_r.at[me - 8 * half],
                    send_sem=send_sem.at[3], recv_sem=recv_sem.at[3],
                    device_id=(2 * chip + half, chan), device_id_type=MESH).start()

        loop(0, 8, one)

        @pl.when(core == half)
        def _():
            pltpu.make_async_copy(
                gf_s.at[pl.ds(2 * (me // 2), 2)], gf_r.at[me - 8 * half], recv_sem.at[3]).start()

    def mixes_out(h):
        def product(index):
            taps = spec_t[index, h * 16 : h * 16 + 16, :]
            return jnp.concatenate(
                [times(taps, spec_p[h, index, 16:32, :], 1.0), times(taps, spec_p[h, index, 0:16, :], -1.0)],
                axis=1)

        def store(g, lanes, value):
            mm_s[h, :, g, :, lanes] = value

        inverse(product, 2, store)
        send_all(4 + h, slot_of(mm_s.at[h]), mm_r.at[h])

    for n in range(6, 16):
        loads[n].wait()
    wait_bytes(taps_r, recv_sem.at[0])
    forward(lambda g, lanes: taps_r[:, g * 16 : g * 16 + 16, lanes], spec_t)
    for h in range(2):
        wait_bytes(pair_r.at[h], recv_sem.at[1 + h])
        forward(lambda g, lanes: pair_r[h, :, g, :, lanes], spec_p.at[h])
        if h == 1:
            filter_out()
        mixes_out(h)

    def activations(h, block, lanes):
        rows = rows_of(block, h)
        skip = wcol[rows, 9:10]
        mixed = mm_r[h, block, 0, :, lanes].astype(F32) + skip * pair_s[h, block, 1, :, lanes].astype(F32)
        grad_mix = mm_r[h, block, 1, :, lanes].astype(F32) + skip * pair_s[h, block, 0, :, lanes].astype(F32)
        return (
            go[rows, lanes].astype(F32) * mixed,
            grad_mix * actv[rows, lanes],
            grad_mix * act2[rows, lanes],
        )

    def edge_copy(h):
        return neighbour(edge_s.at[h], edge_r.at[h], 1 + h, previous)

    def edges_out(h):
        wait_bytes(mm_r.at[h], recv_sem.at[4 + h])

        def body(block):
            for s, value in enumerate(activations(h, block, slice(0, 128))):
                first_tile[s, pl.ds(multiple(block * 16, 16), 16), :] = value.astype(BF16)

        loop(0, 16, body)
        edges = jnp.zeros((16, 256), F32)
        for s in range(3):
            pick = ((row == 2 * s) & (lane == 0)) | ((row == 2 * s + 1) & (lane == 1))
            edges += dot_nt(pick.astype(F32).astype(BF16), first_tile[s])
        edge_s[h] = edges.astype(BF16)
        edge_copy(h).start()

    def adjoint(h):
        edge_copy(h).wait_recv()
        wrow[0:16, 0:256] = edge_r[h].astype(F32) * (me < 15).astype(F32)
        hcol[0:256, :] = jnp.transpose(wrow[:, 0:256])

        def body(block):
            rows = rows_of(block, h)
            weight = wcol[rows, :]
            halo = hcol[pl.ds(multiple(block * 16, 16), 16), :]
            total = jnp.zeros((16, 512), F32)
            fields = activations(h, block, slice(0, 512))
            for s, (field, stream, out) in enumerate(zip(fields, (x1, x2, xv), (o1, o2, ov))):
                next_one, next_two = halo[:, 2 * s : 2 * s + 1], halo[:, 2 * s + 1 : 2 * s + 2]
                one = jnp.where(lane16 == 511, next_one, pltpu.roll(field, 511, 1))
                two = jnp.where(
                    lane16 == 511, next_two, jnp.where(lane16 == 510, next_one, pltpu.roll(field, 510, 1)))
                full = (
                    weight[:, 3 * s : 3 * s + 1] * field
                    + weight[:, 3 * s + 1 : 3 * s + 2] * one
                    + weight[:, 3 * s + 2 : 3 * s + 3] * two
                )
                out[rows, :] = full.astype(BF16)
                total += stream[rows, :].astype(F32) * full
            sal_s[...] += total[0:8] + total[8:16]

        loop(0, 16, body)

    edges_out(0)

    loads[16].wait()
    swap_in = neighbour(sk_h, sk.at[1 - core], 3, sibling)
    swap_in.wait_recv()
    wait_bytes(gf_s, recv_sem.at[3])

    def sketch_rows(block):
        rows = pl.ds(block * 256, 256)
        total = dot_nt(sk[0, rows, :], gf_r[:, 0].reshape(256, 512))
        total += dot_nt(sk[1, rows, :], gf_r[:, 1].reshape(256, 512))
        part_s[pl.ds(block * 4, 4)] = total.astype(BF16).reshape(4, 64, 256)

    unrolled(0, 4, sketch_rows)
    send_all(6, slot_of(part_s), rs_r, 1, 8)
    sal_s[...] = jnp.zeros((8, 512), F32)
    adjoint(0)
    edges_out(1)
    send_all(6, slot_of(part_s), rs_r, 8, 16)
    adjoint(1)
    outs = [
        pltpu.make_async_copy(a, b, out_sem.at[n])
        for n, (a, b) in enumerate(((o1, o1_h), (o2, o2_h), (ov, ov_h), (osk, osk_h), (osal, osal_h)))
    ]
    for n in range(3):
        outs[n].start()

    def sal_send_to(i):
        pltpu.make_async_remote_copy(
            src_ref=sal_s, dst_ref=sal_r.at[chan], send_sem=sal_send.at[0], recv_sem=sal_recv.at[0],
            device_id=(me, lax.rem(chan + i, 8)), device_id_type=MESH).start()

    loop(1, 8, sal_send_to)
    pltpu.make_async_copy(sal_s, sal_r.at[chan], sal_recv.at[0]).start()

    wait_bytes(rs_r, recv_sem.at[6])
    for side in range(2):
        total = rs_r[side].astype(F32)
        for chip in range(1, 8):
            total += rs_r[2 * chip + side].astype(F32)
        osk[:, side * 256 : side * 256 + 256] = total
    outs[3].start()

    wait_bytes(sal_r, sal_recv.at[0])
    total = sal_r[0]
    for n in range(1, 8):
        total += sal_r[n]
    total = jnp.sum(total, axis=0, keepdims=True) * (3.0 * D) ** (-0.5)
    total = jnp.broadcast_to(total, (8, 512))
    osal[...] = pltpu.roll(total, 512 - chan * 64, 1)[:, 0:128]
    outs[4].start()

    tail_copy.wait_send()
    swap.wait_send()
    wait_bytes(taps_r.at[pl.ds(0, 15)], send_sem.at[0])
    for h in range(2):
        edge_copy(h).wait_send()
        wait_bytes(pair_s.at[h, pl.ds(0, 15)], send_sem.at[1 + h])
        wait_bytes(mm_s.at[h, pl.ds(0, 15)], send_sem.at[4 + h])
    wait_bytes(gf_s.at[pl.ds(0, 14)], send_sem.at[3])

    @pl.when(core != half)
    def _():
        wait_bytes(gf_s.at[pl.ds(14, 2)], send_sem.at[3])

    wait_bytes(part_s.at[pl.ds(0, 15)], send_sem.at[6])
    wait_bytes(sal_r.at[pl.ds(0, 7)], sal_send.at[0])
    for out in outs:
        out.wait()


def finish(a1, a2, av, asal, ask, b1, b2, bv, bsal, bsk, c1, c2, cv, ck, in_sem, out_sem):
    stages = ((a1, c1, b1), (a2, c2, b2), (av, cv, bv), (ask, ck, bsk))
    ins = [pltpu.make_async_copy(a, c, in_sem.at[n]) for n, (a, c, _) in enumerate(stages)]
    outs = [pltpu.make_async_copy(c, b, out_sem.at[n]) for n, (_, c, b) in enumerate(stages)]
    for copy in ins:
        copy.start()
    bsal[...] = asal[0, 0:64]
    for first, second in zip(ins, outs):
        first.wait()
        second.start()
    for copy in outs:
        copy.wait()


def on_device(*arrays):
    one, two, value, grad, taps, short, gain, sketch = arrays
    tables = [jnp.asarray(t) for t in host_tables()]
    operands = [one, two, value, grad, taps, short, gain.reshape(1, 512), sketch] + tables

    def vmem(shape, dtype=BF16):
        return pltpu.VMEM(shape, dtype)

    square = (512, 512)
    parts = (2, 16, 2, 16, 512)
    scratch = [
        *[vmem(square) for _ in range(4)], vmem((3, 3, 512), F32), vmem((1, 512), F32), vmem((2, 1024, 512)),
        *[vmem(t.shape, t.dtype) for t in tables],
        vmem((128, 512), F32), vmem((512, 128), F32),
        vmem((16, 512)), vmem((16, 512)), vmem((2, 16, 256)), vmem((2, 16, 256)), vmem((512, 128), F32),
        vmem(square, F32), vmem(square, F32),
        vmem(parts), vmem(parts), vmem((16, 32, 512)),
        vmem((4, 512, 256), F32), vmem((ROWS, 256)), vmem((ROWS, 256)),
        vmem((65, 32, 256), F32), vmem((2, 65, 32, 256), F32), vmem((ROWS, 256), F32),
        vmem((4, 512, 256)), vmem((4, 512, 256)),
        vmem((16, 32, 512)), vmem((8, 2, 32, 512)), vmem(parts), vmem(parts),
        vmem((16, 64, 256)), vmem((16, 64, 256)),
        vmem((3, 256, 128)), vmem((8, 512), F32), vmem((8, 8, 512), F32),
        *[vmem(square) for _ in range(3)], vmem((8, 128), F32), vmem((64, 512), F32),
        pltpu.SemaphoreType.DMA((17,)), pltpu.SemaphoreType.DMA((5,)),
        pltpu.SemaphoreType.DMA((7,)), pltpu.SemaphoreType.DMA((7,)),
        pltpu.SemaphoreType.DMA((4,)), pltpu.SemaphoreType.DMA((4,)),
        pltpu.SemaphoreType.DMA((1,)), pltpu.SemaphoreType.DMA((1,)),
    ]
    results = pl.pallas_call(
        kernel,
        out_shape=[
            *[jax.ShapeDtypeStruct(square, BF16) for _ in range(3)],
            jax.ShapeDtypeStruct((8, 128), F32),
            jax.ShapeDtypeStruct((64, 512), F32),
        ],
        in_specs=[pl.BlockSpec(memory_space=pl.ANY) for _ in operands],
        out_specs=[pl.BlockSpec(memory_space=pl.ANY) for _ in range(5)],
        scratch_shapes=scratch,
        compiler_params=pltpu.CompilerParams(
            collective_id=0, has_side_effects=True, vmem_limit_bytes=56 * 1024 * 1024),
    )(*operands)
    anywhere = pl.BlockSpec(memory_space=pl.ANY)
    near = pl.BlockSpec(memory_space=pltpu.VMEM)
    return pl.pallas_call(
        finish,
        out_shape=[
            *[jax.ShapeDtypeStruct(square, BF16) for _ in range(3)],
            jax.ShapeDtypeStruct((64,), F32),
            jax.ShapeDtypeStruct((64, 512), F32),
        ],
        in_specs=[anywhere, anywhere, anywhere, near, anywhere],
        out_specs=[anywhere, anywhere, anywhere, near, anywhere],
        scratch_shapes=[
            *[vmem(square) for _ in range(3)], vmem((64, 512), F32),
            pltpu.SemaphoreType.DMA((4,)), pltpu.SemaphoreType.DMA((4,)),
        ],
    )(*results)


def solution(mesh):
    return jax.shard_map(
        on_device,
        mesh=mesh,
        in_specs=(
            P("chan", "seq"),
            P("chan", "seq"),
            P("chan", "seq"),
            P("chan", "seq"),
            P("chan", "seq"),
            P(None, None, "chan"),
            P("chan"),
            P(None, "seq"),
        ),
        out_specs=(
            P("chan", "seq"),
            P("chan", "seq"),
            P("chan", "seq"),
            P(("seq", "chan")),
            P("seq", "chan"),
        ),
        check_vma=False,
    )
```

```python
import functools
import math

import jax
import jax.numpy as jnp
import numpy as np
from jax import lax
from jax.experimental import pallas as pl
from jax.experimental.pallas import tpu as pltpu
from jax.sharding import PartitionSpec as P

D = 4096
MESH = pl.DeviceIdType.MESH
F32 = jnp.float32
BF16 = jnp.bfloat16
ROOT = math.sqrt(0.5)
FREQS = [k1 + 32 * q for k1 in range(1, 16) for q in range(4)] + [0, 32, 64, 16, 48]
ROWS = 32 * len(FREQS)


def split_host(table):
    high = table.astype(jnp.bfloat16)
    low = (table - high.astype(np.float64)).astype(jnp.bfloat16)
    return high, low


def host_tables():
    shard = np.arange(16)
    k1 = np.arange(16)
    first = np.zeros((4, 32, 16))
    for tile in range(4):
        angle = 2 * np.pi * np.outer(k1, 4 * shard + tile) / 128
        first[tile, :16] = np.cos(angle)
        first[tile, 16:] = -np.sin(angle)
        first[tile, 16] = (-1.0) ** shard
    eye = np.eye(16)
    wide = np.einsum("tks,cd->tkcsd", first, eye).reshape(4, 512, 256)
    back = np.einsum("tks,cd->tsckd", first, eye).reshape(4, 256, 512) * (2.0 / 16384)
    lane = np.arange(128)
    angle = 2 * np.pi * np.outer(lane, lane) / 128
    cos, sin = np.cos(angle), np.sin(angle)
    inner = np.block([[cos, -sin], [sin, cos]])
    inner_back = np.block([[cos, sin], [-sin, cos]])
    twist = 2 * np.pi * np.outer(np.array(FREQS + [0] * 7), lane) / 16384
    twist = np.concatenate([twist, twist], axis=1)
    return (
        *split_host(wide),
        *split_host(back),
        *split_host(inner),
        *split_host(inner_back),
        np.cos(twist).astype(np.float32),
        np.sin(twist).astype(np.float32),
    )


def dot(left, right):
    return jnp.dot(left, right, preferred_element_type=F32)


def dot_nt(left, right):
    return lax.dot_general(left, right, (((1,), (1,)), ((), ())), preferred_element_type=F32)


def halves(value):
    high = value.astype(BF16)
    return high, (value - high.astype(F32)).astype(BF16)


def multiple(value, of):
    return value if isinstance(value, int) else pl.multiple_of(value, of)


def unrolled(first, last, body):
    for index in range(first, last):
        body(index)


def loop(first, last, body):
    def step(index, carry):
        body(index)
        return carry

    lax.fori_loop(first, last, step, 0)


def kernel(
    x1_h, x2_h, xv_h, go_h, taps_h, short_h, gain_h, sk_h,
    c1h_h, c1l_h, dh_h, dl_h, mh_h, ml_h, nh_h, nl_h, twc_h, tws_h,
    o1_h, o2_h, ov_h, osal_h, osk_h,
    x1, x2, xv, go, short, gain, sk,
    c1h, c1l, dh, dl, mh, ml, nh, nl, twc, tws,
    wrow, wcol, tail_s, tail_r, head_s, head_r, hcol, head_tile, head_gate, head_mult,
    act2, actv,
    pair_s, pair_r, taps_r,
    y, zh, zl, spec_t, spec_p, e, wh, wl,
    gf_s, gf_r, mm_s, mm_r,
    part_s, rs_r, sal_s, sal_r, o1, o2, ov, osal, osk,
    load_sem, out_sem, send_sem, recv_sem, halo_send, halo_recv, sal_send, sal_recv,
):
    me = lax.axis_index("seq")
    chan = lax.axis_index("chan")
    core = lax.rem(me, 2)
    half = me // 8
    sibling = me + 1 - 2 * core
    following = lax.rem(me + 1, 16)
    previous = lax.rem(me + 15, 16)

    loads = [
        (x1_h, x1), (x2_h, x2), (xv_h, xv), (go_h, go), (short_h, short), (gain_h, gain),
        (c1h_h, c1h), (c1l_h, c1l), (mh_h, mh), (ml_h, ml), (twc_h, twc), (tws_h, tws),
        (nh_h, nh), (nl_h, nl), (dh_h, dh), (dl_h, dl), (sk_h, sk.at[core]),
    ]
    loads = [pltpu.make_async_copy(a, b, load_sem.at[n]) for n, (a, b) in enumerate(loads)]
    for load in loads:
        load.start()

    barrier = pltpu.get_barrier_semaphore()
    loop(1, 16, lambda i: pl.semaphore_signal(
        barrier, inc=1, device_id=(lax.rem(me + i, 16), chan), device_id_type=MESH))
    loop(1, 8, lambda i: pl.semaphore_signal(
        barrier, inc=1, device_id=(me, lax.rem(chan + i, 8)), device_id_type=MESH))

    def block_of(ref):
        return lambda to: ref.at[pl.ds(multiple(to * 32, 32), 32)]

    def slot_of(ref):
        return lambda to: ref.at[to]

    def send_all(kind, source, target, begin=1, end=16):
        def one(i):
            to = lax.rem(me + i, 16)
            pltpu.make_async_remote_copy(
                src_ref=source(to), dst_ref=target.at[me],
                send_sem=send_sem.at[kind], recv_sem=recv_sem.at[kind],
                device_id=(to, chan), device_id_type=MESH,
            ).start()

        loop(begin, end, one)
        if end == 16:
            pltpu.make_async_copy(source(me), target.at[me], recv_sem.at[kind]).start()

    def wait_bytes(ref, sem):
        pltpu.make_async_copy(ref, ref, sem).wait()

    def neighbour(source, target, n, to):
        return pltpu.make_async_remote_copy(
            src_ref=source, dst_ref=target, send_sem=halo_send.at[n], recv_sem=halo_recv.at[n],
            device_id=(to, chan), device_id_type=MESH)

    pl.semaphore_wait(barrier, 22)
    send_all(0, block_of(taps_h), taps_r, 1, 7)

    for n in range(3):
        loads[n].wait()
    row = lax.broadcasted_iota(jnp.int32, (16, 128), 0)
    lane = lax.broadcasted_iota(jnp.int32, (16, 128), 1)
    tails = jnp.zeros((16, 512), F32)
    for s, ref in enumerate((x1, x2, xv)):
        pick = ((row == 2 * s) & (lane == 126)) | ((row == 2 * s + 1) & (lane == 127))
        tails += dot_nt(pick.astype(F32).astype(BF16), ref[:, 384:512])
    tail_s[...] = tails.astype(BF16)
    tail_copy = neighbour(tail_s, tail_r, 0, following)
    tail_copy.start()
    send_all(0, block_of(taps_h), taps_r, 7, 16)
    for n in range(3, 6):
        loads[n].wait()

    wrow[...] = jnp.zeros((128, 512), F32)
    for s in range(3):
        wrow[3 * s : 3 * s + 3, :] = short[s]
    wrow[9:10, :] = gain[...]
    wcol[...] = jnp.transpose(wrow[...])

    tail_copy.wait_recv()
    wrow[0:16, :] = tail_r[...].astype(F32) * (me > 0).astype(F32)
    hcol[...] = jnp.transpose(wrow[...])

    lane16 = lax.broadcasted_iota(jnp.int32, (16, 512), 1)

    def rows_of(block, h):
        return pl.ds(multiple(block * 32 + h * 16, 16), 16)

    def gate(h):
        def body(block):
            rows = rows_of(block, h)
            weight = wcol[rows, :]
            halo = hcol[rows, :]

            def short_filter(ref, s):
                field = ref[rows, :].astype(F32)
                before, last = halo[:, 2 * s : 2 * s + 1], halo[:, 2 * s + 1 : 2 * s + 2]
                one = jnp.where(lane16 == 0, last, pltpu.roll(field, 1, 1))
                two = jnp.where(lane16 == 0, before, jnp.where(lane16 == 1, last, pltpu.roll(field, 2, 1)))
                return (
                    weight[:, 3 * s : 3 * s + 1] * field
                    + weight[:, 3 * s + 1 : 3 * s + 2] * one
                    + weight[:, 3 * s + 2 : 3 * s + 3] * two
                )

            first = short_filter(x1, 0)
            grad = go[rows, :]
            pair_s[h, block, 0] = (grad.astype(F32) * first).astype(BF16)
            second = short_filter(x2, 1)
            value = short_filter(xv, 2)
            act2[rows, :] = second
            actv[rows, :] = value
            pair_s[h, block, 1] = (second * value).astype(BF16)
            spot = pl.ds(multiple(block * 16, 16), 16)
            head_tile[h, 0, spot, :] = pair_s[h, block, 1, :, 0:128]
            head_tile[h, 1, spot, :] = pair_s[h, block, 0, :, 0:128]
            head_tile[h, 2, spot, :] = grad[:, 0:128]
            head_tile[h, 3, spot, :] = value[:, 0:128].astype(BF16)
            head_tile[h, 4, spot, :] = second[:, 0:128].astype(BF16)

        loop(0, 16, body)

    for h in range(2):
        gate(h)
        send_all(1 + h, slot_of(pair_s.at[h]), pair_r.at[h])
    swap = neighbour(sk_h, sk.at[core], 2, sibling)
    swap.start()

    for h in range(2):
        heads = jnp.zeros((16, 256), F32)
        for at, n in ((0, 0), (2, 1), (4, 1), (6, 2), (8, 3), (10, 4)):
            pick = ((row == at) & (lane == 0)) | ((row == at + 1) & (lane == 1))
            heads += dot_nt(pick.astype(F32).astype(BF16), head_tile[h, n])
        head_s[h] = heads.astype(BF16)
    head_copy = neighbour(head_s, head_r, 1, previous)
    head_copy.start()

    def first_rows(tile, part, k1):
        return y[tile, pl.ds(multiple(part * 256 + k1 * 16, 16), 16), :]

    def store_z(index, re, im):
        for g in range(2):
            rows = pl.ds(multiple(index * 32 + g * 16, 16), 16)
            side = slice(g * 128, g * 128 + 128)
            high, low = halves(jnp.concatenate([re[:, side], im[:, side]], axis=1))
            zh[rows, :] = high
            zl[rows, :] = low

    def twist(index, re, im):
        cos, sin = twc[pl.ds(index, 1), :], tws[pl.ds(index, 1), :]
        store_z(index, re * cos + im * sin, im * cos - re * sin)

    def forward(source, spec):
        def stage(tile):
            lanes = pl.ds(multiple(tile * 128, 128), 128)
            right = jnp.concatenate([source(g, lanes).reshape(256, 128) for g in range(2)], axis=1)
            y[tile] = dot(c1h[tile], right) + dot(c1l[tile], right)

        unrolled(0, 4, stage)

        def butterfly(k1):
            r0, r1, r2, r3 = [first_rows(t, 0, k1) for t in range(4)]
            i0, i1, i2, i3 = [first_rows(t, 1, k1) for t in range(4)]
            ar, ai, br, bi = r0 + r2, i0 + i2, r0 - r2, i0 - i2
            cr, ci, dr, di = r1 + r3, i1 + i3, r1 - r3, i1 - i3
            base = (k1 - 1) * 4
            twist(base, ar + cr, ai + ci)
            twist(base + 1, br + di, bi - dr)
            twist(base + 2, ar - cr, ai - ci)
            twist(base + 3, br - di, bi + dr)

        unrolled(1, 16, butterfly)
        r0, r1, r2, r3 = [first_rows(t, 0, 0) for t in range(4)]
        none = jnp.zeros_like(r0)
        store_z(60, r0 + r1 + r2 + r3, none)
        twist(61, r0 - r2, r3 - r1)
        twist(62, r0 - r1 + r2 - r3, none)
        r0, r1, r2, r3 = [first_rows(t, 1, 0) for t in range(4)]
        twist(63, r0 + ROOT * (r1 - r3), -r2 - ROOT * (r1 + r3))
        twist(64, r0 - ROOT * (r1 - r3), r2 - ROOT * (r1 + r3))

        def last(chunk):
            rows = pl.ds(multiple(chunk * 416, 16), 416)
            out = dot(zh[rows, :], mh[...]) + dot(zl[rows, :], mh[...]) + dot(zh[rows, :], ml[...])
            spec[pl.ds(chunk * 13, 13)] = out.reshape(13, 32, 256)

        unrolled(0, 5, last)

    def times(left, right, sign):
        lr, li = left[..., 0:128], left[..., 128:256] * sign
        rr, ri = right[..., 0:128], right[..., 128:256]
        return jnp.concatenate([lr * rr - li * ri, lr * ri + li * rr], axis=2)

    def inverse(product, count, store, more=None):
        size = 16 * count
        wide = 128 * count

        def first(chunk):
            high, low = halves(product(pl.ds(chunk * 13, 13)).reshape(13 * size, 256))
            rows = pl.ds(multiple(chunk * 13 * size, 16), 13 * size)
            e[rows, :] = dot(high, nh[...]) + dot(low, nh[...]) + dot(high, nl[...])

        unrolled(0, 5, first)

        def untwist(index):
            cos, sin = twc[pl.ds(index, 1), :][:, 0:wide], tws[pl.ds(index, 1), :][:, 0:wide]
            parts = [e[pl.ds(multiple(index * size + 16 * g, 16), 16), :] for g in range(count)]
            re = jnp.concatenate([p[:, 0:128] for p in parts], axis=1)
            im = jnp.concatenate([p[:, 128:256] for p in parts], axis=1)
            return re * cos - im * sin, im * cos + re * sin

        def store_w(tile, part, k1, value):
            rows = pl.ds(multiple(part * 256 + k1 * 16, 16), 16)
            high, low = halves(value)
            wh[tile, rows, 0:wide] = high
            wl[tile, rows, 0:wide] = low

        def butterfly(k1):
            base = (k1 - 1) * 4
            (r0, i0), (r1, i1), (r2, i2), (r3, i3) = [untwist(base + q) for q in range(4)]
            ar, ai, br, bi = r0 + r2, i0 + i2, r0 - r2, i0 - i2
            cr, ci, dr, di = r1 + r3, i1 + i3, r1 - r3, i1 - i3
            store_w(0, 0, k1, ar + cr)
            store_w(0, 1, k1, ai + ci)
            store_w(1, 0, k1, br - di)
            store_w(1, 1, k1, bi + dr)
            store_w(2, 0, k1, ar - cr)
            store_w(2, 1, k1, ai - ci)
            store_w(3, 0, k1, br + di)
            store_w(3, 1, k1, bi - dr)

        unrolled(1, 16, butterfly)
        (r0, _), (r32, i32), (r64, _), (r16, i16), (r48, i48) = [untwist(60 + n) for n in range(5)]
        plus, minus = 0.5 * (r0 + r64), 0.5 * (r0 - r64)
        store_w(0, 0, 0, plus + r32)
        store_w(1, 0, 0, minus - i32)
        store_w(2, 0, 0, plus - r32)
        store_w(3, 0, 0, minus + i32)
        store_w(0, 1, 0, r16 + r48)
        store_w(1, 1, 0, ROOT * (r16 - i16 - r48 - i48))
        store_w(2, 1, 0, i48 - i16)
        store_w(3, 1, 0, ROOT * (r48 - i48 - r16 - i16))

        def last(tile):
            high, low = wh[tile, :, 0:wide], wl[tile, :, 0:wide]
            out = dot(dh[tile], high) + dot(dh[tile], low) + dot(dl[tile], high)
            for g in range(count):
                store(g, tile, out[:, g * 128 : g * 128 + 128].astype(BF16).reshape(16, 16, 128))
            if more is not None and tile == 0:
                more(out)

        unrolled(0, 4, last)

    def filter_out():
        def product(index):
            return jnp.concatenate(
                [times(spec_p[h, index, 16:32, :], spec_p[h, index, 0:16, :], -1.0) for h in range(2)],
                axis=1)

        def store(g, tile, value):
            gf_s[:, g * 16 : g * 16 + 16, tile * 128 : tile * 128 + 128] = value

        inverse(product, 2, store)

        def one(n):
            chip = lax.rem(me // 2 + n, 8)

            @pl.when(2 * chip + half != me)
            def _():
                pltpu.make_async_remote_copy(
                    src_ref=gf_s.at[pl.ds(2 * chip, 2)], dst_ref=gf_r.at[me - 8 * half],
                    send_sem=send_sem.at[3], recv_sem=recv_sem.at[3],
                    device_id=(2 * chip + half, chan), device_id_type=MESH).start()

        loop(0, 8, one)

        @pl.when(core == half)
        def _():
            pltpu.make_async_copy(
                gf_s.at[pl.ds(2 * (me // 2), 2)], gf_r.at[me - 8 * half], recv_sem.at[3]).start()

    def mixes_out(h):
        def product(index):
            taps = spec_t[index, h * 16 : h * 16 + 16, :]
            return jnp.concatenate(
                [times(taps, spec_p[h, index, 16:32, :], 1.0), times(taps, spec_p[h, index, 0:16, :], -1.0)],
                axis=1)

        def store(g, tile, value):
            mm_s[h, :, 4 * g + tile] = value

        def more(out):
            mixed, grad_mix = out[16:256, 0:128], out[16:256, 128:256]
            side = lax.broadcasted_iota(jnp.int32, (240, 128), 1)
            value = jnp.where(side < 2, mixed, jnp.where(side < 4, pltpu.roll(grad_mix, 2, 1), pltpu.roll(grad_mix, 4, 1)))
            mm_s[h, 0:15, 8] = value.astype(BF16).reshape(15, 16, 128)
            mm_s[h, 15, 8] = jnp.zeros((16, 128), BF16)

        inverse(product, 2, store, more)
        send_all(4 + h, slot_of(mm_s.at[h]), mm_r.at[h])

    for n in range(6, 16):
        loads[n].wait()
    wait_bytes(taps_r, recv_sem.at[0])
    forward(lambda g, lanes: taps_r[:, g * 16 : g * 16 + 16, lanes], spec_t)
    for h in range(2):
        wait_bytes(pair_r.at[h], recv_sem.at[1 + h])
        forward(lambda g, lanes: pair_r[h, :, g, :, lanes], spec_p.at[h])
        if h == 1:
            filter_out()
        mixes_out(h)

    def adjoint(h):
        wait_bytes(mm_r.at[h], recv_sem.at[4 + h])

        def body(block):
            rows = rows_of(block, h)
            weight = wcol[rows, :]
            skip = weight[:, 9:10]
            spot = pl.ds(multiple(block * 16, 16), 16)
            halo = head_mult[h, spot, :] * (mm_r[h, block, 8].astype(F32) + skip * head_gate[h, spot, :])
            mixed, grad_mix = [
                jnp.concatenate([mm_r[h, block, 4 * g + tile] for tile in range(4)], axis=1).astype(F32)
                + skip * pair_s[h, block, 1 - g].astype(F32)
                for g in range(2)
            ]
            fields = (go[rows, :].astype(F32) * mixed, grad_mix * actv[rows, :], grad_mix * act2[rows, :])
            total = jnp.zeros((16, 512), F32)
            for s, (field, stream, out) in enumerate(zip(fields, (x1, x2, xv), (o1, o2, ov))):
                next_one, next_two = halo[:, 2 * s : 2 * s + 1], halo[:, 2 * s + 1 : 2 * s + 2]
                one = jnp.where(lane16 == 511, next_one, pltpu.roll(field, 511, 1))
                two = jnp.where(
                    lane16 == 511, next_two, jnp.where(lane16 == 510, next_one, pltpu.roll(field, 510, 1)))
                full = (
                    weight[:, 3 * s : 3 * s + 1] * field
                    + weight[:, 3 * s + 1 : 3 * s + 2] * one
                    + weight[:, 3 * s + 2 : 3 * s + 3] * two
                )
                out[rows, :] = full.astype(BF16)
                total += stream[rows, :].astype(F32) * full
            sal_s[...] += total[0:8] + total[8:16]

        loop(0, 16, body)

    loads[16].wait()
    swap_in = neighbour(sk_h, sk.at[1 - core], 2, sibling)
    swap_in.wait_recv()
    wait_bytes(gf_s, recv_sem.at[3])

    def sketch_rows(block):
        rows = pl.ds(block * 256, 256)
        total = dot_nt(sk[0, rows, :], gf_r[:, 0].reshape(256, 512))
        total += dot_nt(sk[1, rows, :], gf_r[:, 1].reshape(256, 512))
        part_s[pl.ds(block * 4, 4)] = total.astype(BF16).reshape(4, 64, 256)

    unrolled(0, 4, sketch_rows)
    send_all(6, slot_of(part_s), rs_r)
    sal_s[...] = jnp.zeros((8, 512), F32)
    head_copy.wait_recv()
    for h in range(2):
        heads = head_r[h].astype(F32) * (me < 15).astype(F32)
        wrow[0:16, 0:256] = heads
        head_gate[h] = jnp.transpose(wrow[:, 0:256])
        wrow[0:16, 0:256] = pltpu.roll(heads, 10, 0)
        head_mult[h] = jnp.transpose(wrow[:, 0:256])
    adjoint(0)
    adjoint(1)
    outs = [
        pltpu.make_async_copy(a, b, out_sem.at[n])
        for n, (a, b) in enumerate(((o1, o1_h), (o2, o2_h), (ov, ov_h), (osk, osk_h), (osal, osal_h)))
    ]
    for n in range(3):
        outs[n].start()

    def sal_send_to(i):
        pltpu.make_async_remote_copy(
            src_ref=sal_s, dst_ref=sal_r.at[chan], send_sem=sal_send.at[0], recv_sem=sal_recv.at[0],
            device_id=(me, lax.rem(chan + i, 8)), device_id_type=MESH).start()

    loop(1, 8, sal_send_to)
    pltpu.make_async_copy(sal_s, sal_r.at[chan], sal_recv.at[0]).start()

    wait_bytes(rs_r, recv_sem.at[6])
    for side in range(2):
        total = rs_r[side].astype(F32)
        for chip in range(1, 8):
            total += rs_r[2 * chip + side].astype(F32)
        osk[:, side * 256 : side * 256 + 256] = total
    outs[3].start()

    wait_bytes(sal_r, sal_recv.at[0])
    total = sal_r[0]
    for n in range(1, 8):
        total += sal_r[n]
    total = jnp.sum(total, axis=0, keepdims=True) * (3.0 * D) ** (-0.5)
    total = jnp.broadcast_to(total, (8, 512))
    osal[...] = pltpu.roll(total, 512 - chan * 64, 1)[:, 0:128]
    outs[4].start()

    tail_copy.wait_send()
    swap.wait_send()
    head_copy.wait_send()
    wait_bytes(taps_r.at[pl.ds(0, 15)], send_sem.at[0])
    for h in range(2):
        wait_bytes(pair_s.at[h, pl.ds(0, 15)], send_sem.at[1 + h])
        wait_bytes(mm_s.at[h, pl.ds(0, 15)], send_sem.at[4 + h])
    wait_bytes(gf_s.at[pl.ds(0, 14)], send_sem.at[3])

    @pl.when(core != half)
    def _():
        wait_bytes(gf_s.at[pl.ds(14, 2)], send_sem.at[3])

    wait_bytes(part_s.at[pl.ds(0, 15)], send_sem.at[6])
    wait_bytes(sal_r.at[pl.ds(0, 7)], sal_send.at[0])
    for out in outs:
        out.wait()


def finish(a1, a2, av, asal, ask, b1, b2, bv, bsal, bsk, c1, c2, cv, ck, in_sem, out_sem):
    stages = ((a1, c1, b1), (a2, c2, b2), (av, cv, bv), (ask, ck, bsk))
    ins = [pltpu.make_async_copy(a, c, in_sem.at[n]) for n, (a, c, _) in enumerate(stages)]
    outs = [pltpu.make_async_copy(c, b, out_sem.at[n]) for n, (_, c, b) in enumerate(stages)]
    for copy in ins:
        copy.start()
    bsal[...] = asal[0, 0:64]
    for first, second in zip(ins, outs):
        first.wait()
        second.start()
    for copy in outs:
        copy.wait()


def on_device(*arrays):
    one, two, value, grad, taps, short, gain, sketch = arrays
    tables = [jnp.asarray(t) for t in host_tables()]
    operands = [one, two, value, grad, taps, short, gain.reshape(1, 512), sketch] + tables

    def vmem(shape, dtype=BF16):
        return pltpu.VMEM(shape, dtype)

    square = (512, 512)
    parts = (2, 16, 2, 16, 512)
    mixes = (2, 16, 9, 16, 128)
    scratch = [
        *[vmem(square) for _ in range(4)], vmem((3, 3, 512), F32), vmem((1, 512), F32), vmem((2, 1024, 512)),
        *[vmem(t.shape, t.dtype) for t in tables],
        vmem((128, 512), F32), vmem((512, 128), F32),
        vmem((16, 512)), vmem((16, 512)), vmem((2, 16, 256)), vmem((2, 16, 256)), vmem((512, 128), F32),
        vmem((2, 5, 256, 128)), vmem((2, 256, 128), F32), vmem((2, 256, 128), F32),
        vmem(square, F32), vmem(square, F32),
        vmem(parts), vmem(parts), vmem((16, 32, 512)),
        vmem((4, 512, 256), F32), vmem((ROWS, 256)), vmem((ROWS, 256)),
        vmem((65, 32, 256), F32), vmem((2, 65, 32, 256), F32), vmem((ROWS, 256), F32),
        vmem((4, 512, 256)), vmem((4, 512, 256)),
        vmem((16, 32, 512)), vmem((8, 2, 32, 512)), vmem(mixes), vmem(mixes),
        vmem((16, 64, 256)), vmem((16, 64, 256)),
        vmem((8, 512), F32), vmem((8, 8, 512), F32),
        *[vmem(square) for _ in range(3)], vmem((8, 128), F32), vmem((64, 512), F32),
        pltpu.SemaphoreType.DMA((17,)), pltpu.SemaphoreType.DMA((5,)),
        pltpu.SemaphoreType.DMA((7,)), pltpu.SemaphoreType.DMA((7,)),
        pltpu.SemaphoreType.DMA((3,)), pltpu.SemaphoreType.DMA((3,)),
        pltpu.SemaphoreType.DMA((1,)), pltpu.SemaphoreType.DMA((1,)),
    ]
    results = pl.pallas_call(
        kernel,
        out_shape=[
            *[jax.ShapeDtypeStruct(square, BF16) for _ in range(3)],
            jax.ShapeDtypeStruct((8, 128), F32),
            jax.ShapeDtypeStruct((64, 512), F32),
        ],
        in_specs=[pl.BlockSpec(memory_space=pl.ANY) for _ in operands],
        out_specs=[pl.BlockSpec(memory_space=pl.ANY) for _ in range(5)],
        scratch_shapes=scratch,
        compiler_params=pltpu.CompilerParams(
            collective_id=0, has_side_effects=True, vmem_limit_bytes=56 * 1024 * 1024),
    )(*operands)
    anywhere = pl.BlockSpec(memory_space=pl.ANY)
    near = pl.BlockSpec(memory_space=pltpu.VMEM)
    return pl.pallas_call(
        finish,
        out_shape=[
            *[jax.ShapeDtypeStruct(square, BF16) for _ in range(3)],
            jax.ShapeDtypeStruct((64,), F32),
            jax.ShapeDtypeStruct((64, 512), F32),
        ],
        in_specs=[anywhere, anywhere, anywhere, near, anywhere],
        out_specs=[anywhere, anywhere, anywhere, near, anywhere],
        scratch_shapes=[
            *[vmem(square) for _ in range(3)], vmem((64, 512), F32),
            pltpu.SemaphoreType.DMA((4,)), pltpu.SemaphoreType.DMA((4,)),
        ],
    )(*results)


def solution(mesh):
    return jax.shard_map(
        on_device,
        mesh=mesh,
        in_specs=(
            P("chan", "seq"),
            P("chan", "seq"),
            P("chan", "seq"),
            P("chan", "seq"),
            P("chan", "seq"),
            P(None, None, "chan"),
            P("chan"),
            P(None, "seq"),
        ),
        out_specs=(
            P("chan", "seq"),
            P("chan", "seq"),
            P("chan", "seq"),
            P(("seq", "chan")),
            P("seq", "chan"),
        ),
        check_vma=False,
    )
```

```python
import functools
import math

import jax
import jax.numpy as jnp
import numpy as np
from jax import lax
from jax.experimental import pallas as pl
from jax.experimental.pallas import tpu as pltpu
from jax.sharding import PartitionSpec as P

D = 4096
MESH = pl.DeviceIdType.MESH
F32 = jnp.float32
BF16 = jnp.bfloat16
ROOT = math.sqrt(0.5)
FREQS = [k1 + 32 * q for k1 in range(1, 16) for q in range(4)] + [0, 32, 64, 16, 48]
ROWS = 32 * len(FREQS)


def split_host(table):
    high = table.astype(jnp.bfloat16)
    low = (table - high.astype(np.float64)).astype(jnp.bfloat16)
    return high, low


def host_tables():
    shard = np.arange(16)
    k1 = np.arange(16)
    first = np.zeros((4, 32, 16))
    for tile in range(4):
        angle = 2 * np.pi * np.outer(k1, 4 * shard + tile) / 128
        first[tile, :16] = np.cos(angle)
        first[tile, 16:] = -np.sin(angle)
        first[tile, 16] = (-1.0) ** shard
    eye = np.eye(16)
    wide = np.einsum("tks,cd->tkcsd", first, eye).reshape(4, 512, 256)
    back = np.einsum("tks,cd->tsckd", first, eye).reshape(4, 256, 512) * (2.0 / 16384)
    lane = np.arange(128)
    angle = 2 * np.pi * np.outer(lane, lane) / 128
    cos, sin = np.cos(angle), np.sin(angle)
    inner = np.block([[cos, -sin], [sin, cos]])
    inner_back = np.block([[cos, sin], [-sin, cos]])
    twist = 2 * np.pi * np.outer(np.array(FREQS + [0] * 7), lane) / 16384
    twist = np.concatenate([twist, twist], axis=1)
    return (
        *split_host(wide),
        *split_host(back),
        *split_host(inner),
        *split_host(inner_back),
        np.cos(twist).astype(np.float32),
        np.sin(twist).astype(np.float32),
    )


def dot(left, right):
    return jnp.dot(left, right, preferred_element_type=F32)


def dot_nt(left, right):
    return lax.dot_general(left, right, (((1,), (1,)), ((), ())), preferred_element_type=F32)


def halves(value):
    high = value.astype(BF16)
    return high, (value - high.astype(F32)).astype(BF16)


def multiple(value, of):
    return value if isinstance(value, int) else pl.multiple_of(value, of)


def unrolled(first, last, body):
    for index in range(first, last):
        body(index)


def loop(first, last, body):
    def step(index, carry):
        body(index)
        return carry

    lax.fori_loop(first, last, step, 0)


def kernel(
    x1_h, x2_h, xv_h, go_h, taps_h, short_h, gain_h, sk_h,
    c1h_h, c1l_h, dh_h, dl_h, mh_h, ml_h, nh_h, nl_h, twc_h, tws_h,
    o1_h, o2_h, ov_h, osal_h, osk_h,
    x1, x2, xv, go, short, gain, sk,
    c1h, c1l, dh, dl, mh, ml, nh, nl, twc, tws,
    wrow, wcol, tail_s, tail_r, head_s, head_r, hcol, head_tile, head_gate, head_mult,
    act2, actv,
    pair_s, pair_r, taps_r,
    y, zh, zl, spec_t, spec_p, e, wh, wl,
    gf_s, gf_r, mm_s, mm_r,
    part_s, rs_r, sal_s, sal_r, o1, o2, ov, osal, osk,
    load_sem, out_sem, send_sem, recv_sem, halo_send, halo_recv, sal_send, sal_recv,
):
    me = lax.axis_index("seq")
    chan = lax.axis_index("chan")
    core = lax.rem(me, 2)
    half = me // 8
    sibling = me + 1 - 2 * core
    following = lax.rem(me + 1, 16)
    previous = lax.rem(me + 15, 16)

    loads = [
        (x1_h, x1), (x2_h, x2), (xv_h, xv), (go_h, go), (short_h, short), (gain_h, gain),
        (c1h_h, c1h), (c1l_h, c1l), (mh_h, mh), (ml_h, ml), (twc_h, twc), (tws_h, tws),
        (nh_h, nh), (nl_h, nl), (dh_h, dh), (dl_h, dl), (sk_h, sk.at[core]),
    ]
    loads = [pltpu.make_async_copy(a, b, load_sem.at[n]) for n, (a, b) in enumerate(loads)]
    for load in loads:
        load.start()

    barrier = pltpu.get_barrier_semaphore()
    loop(1, 16, lambda i: pl.semaphore_signal(
        barrier, inc=1, device_id=(lax.rem(me + i, 16), chan), device_id_type=MESH))
    loop(1, 8, lambda i: pl.semaphore_signal(
        barrier, inc=1, device_id=(me, lax.rem(chan + i, 8)), device_id_type=MESH))

    def block_of(ref):
        return lambda to: ref.at[pl.ds(multiple(to * 32, 32), 32)]

    def slot_of(ref):
        return lambda to: ref.at[to]

    def send_all(kind, source, target):
        def one(i):
            to = lax.rem(me + i, 16)
            pltpu.make_async_remote_copy(
                src_ref=source(to), dst_ref=target.at[me],
                send_sem=send_sem.at[kind], recv_sem=recv_sem.at[kind],
                device_id=(to, chan), device_id_type=MESH,
            ).start()

        loop(1, 16, one)
        pltpu.make_async_copy(source(me), target.at[me], recv_sem.at[kind]).start()

    def wait_bytes(ref, sem):
        pltpu.make_async_copy(ref, ref, sem).wait()

    def neighbour(source, target, n, to):
        return pltpu.make_async_remote_copy(
            src_ref=source, dst_ref=target, send_sem=halo_send.at[n], recv_sem=halo_recv.at[n],
            device_id=(to, chan), device_id_type=MESH)

    for n in range(3):
        loads[n].wait()
    row = lax.broadcasted_iota(jnp.int32, (16, 128), 0)
    lane = lax.broadcasted_iota(jnp.int32, (16, 128), 1)
    tails = jnp.zeros((16, 512), F32)
    for s, ref in enumerate((x1, x2, xv)):
        pick = ((row == 2 * s) & (lane == 126)) | ((row == 2 * s + 1) & (lane == 127))
        tails += dot_nt(pick.astype(F32).astype(BF16), ref[:, 384:512])
    tail_s[...] = tails.astype(BF16)

    pl.semaphore_wait(barrier, 22)
    tail_copy = neighbour(tail_s, tail_r, 0, following)
    tail_copy.start()
    send_all(0, block_of(taps_h), taps_r)
    for n in range(3, 6):
        loads[n].wait()

    wrow[...] = jnp.zeros((128, 512), F32)
    for s in range(3):
        wrow[3 * s : 3 * s + 3, :] = short[s]
    wrow[9:10, :] = gain[...]
    wcol[...] = jnp.transpose(wrow[...])

    tail_copy.wait_recv()
    wrow[0:16, :] = tail_r[...].astype(F32) * (me > 0).astype(F32)
    hcol[...] = jnp.transpose(wrow[...])

    lane16 = lax.broadcasted_iota(jnp.int32, (16, 512), 1)

    def rows_of(block, h):
        return pl.ds(multiple(block * 32 + h * 16, 16), 16)

    def gate(h):
        def body(block):
            rows = rows_of(block, h)
            weight = wcol[rows, :]
            halo = hcol[rows, :]

            def short_filter(ref, s):
                field = ref[rows, :].astype(F32)
                before, last = halo[:, 2 * s : 2 * s + 1], halo[:, 2 * s + 1 : 2 * s + 2]
                one = jnp.where(lane16 == 0, last, pltpu.roll(field, 1, 1))
                two = jnp.where(lane16 == 0, before, jnp.where(lane16 == 1, last, pltpu.roll(field, 2, 1)))
                return (
                    weight[:, 3 * s : 3 * s + 1] * field
                    + weight[:, 3 * s + 1 : 3 * s + 2] * one
                    + weight[:, 3 * s + 2 : 3 * s + 3] * two
                )

            first = short_filter(x1, 0)
            grad = go[rows, :]
            grad_gate = (grad.astype(F32) * first).astype(BF16)
            pair_s[h, block, 0] = grad_gate
            second = short_filter(x2, 1)
            value = short_filter(xv, 2)
            act2[rows, :] = second
            actv[rows, :] = value
            gated = (second * value).astype(BF16)
            pair_s[h, block, 1] = gated
            spot = pl.ds(multiple(block * 16, 16), 16)
            head_tile[h, 0, spot, :] = gated[:, 0:128]
            head_tile[h, 1, spot, :] = grad_gate[:, 0:128]
            head_tile[h, 2, spot, :] = grad[:, 0:128]
            head_tile[h, 3, spot, :] = value[:, 0:128].astype(BF16)
            head_tile[h, 4, spot, :] = second[:, 0:128].astype(BF16)

        unrolled(0, 16, body)

    for h in range(2):
        gate(h)
        send_all(1 + h, slot_of(pair_s.at[h]), pair_r.at[h])
    swap = neighbour(sk_h, sk.at[core], 2, sibling)
    swap.start()

    for h in range(2):
        heads = jnp.zeros((16, 256), F32)
        for at, n in ((0, 0), (2, 1), (4, 1), (6, 2), (8, 3), (10, 4)):
            pick = ((row == at) & (lane == 0)) | ((row == at + 1) & (lane == 1))
            heads += dot_nt(pick.astype(F32).astype(BF16), head_tile[h, n])
        head_s[h] = heads.astype(BF16)
    head_copy = neighbour(head_s, head_r, 1, previous)
    head_copy.start()

    def first_rows(tile, part, k1):
        return y[tile, pl.ds(multiple(part * 256 + k1 * 16, 16), 16), :]

    def store_z(index, re, im):
        for g in range(2):
            rows = pl.ds(multiple(index * 32 + g * 16, 16), 16)
            side = slice(g * 128, g * 128 + 128)
            high, low = halves(jnp.concatenate([re[:, side], im[:, side]], axis=1))
            zh[rows, :] = high
            zl[rows, :] = low

    def twist(index, re, im):
        cos, sin = twc[pl.ds(index, 1), :], tws[pl.ds(index, 1), :]
        store_z(index, re * cos + im * sin, im * cos - re * sin)

    def forward(source, spec):
        def stage(tile):
            lanes = pl.ds(multiple(tile * 128, 128), 128)
            right = jnp.concatenate([source(g, lanes).reshape(256, 128) for g in range(2)], axis=1)
            y[tile] = dot(c1h[tile], right) + dot(c1l[tile], right)

        unrolled(0, 4, stage)

        def butterfly(k1):
            r0, r1, r2, r3 = [first_rows(t, 0, k1) for t in range(4)]
            i0, i1, i2, i3 = [first_rows(t, 1, k1) for t in range(4)]
            ar, ai, br, bi = r0 + r2, i0 + i2, r0 - r2, i0 - i2
            cr, ci, dr, di = r1 + r3, i1 + i3, r1 - r3, i1 - i3
            base = (k1 - 1) * 4
            twist(base, ar + cr, ai + ci)
            twist(base + 1, br + di, bi - dr)
            twist(base + 2, ar - cr, ai - ci)
            twist(base + 3, br - di, bi + dr)

        unrolled(1, 16, butterfly)
        r0, r1, r2, r3 = [first_rows(t, 0, 0) for t in range(4)]
        none = jnp.zeros_like(r0)
        store_z(60, r0 + r1 + r2 + r3, none)
        twist(61, r0 - r2, r3 - r1)
        twist(62, r0 - r1 + r2 - r3, none)
        r0, r1, r2, r3 = [first_rows(t, 1, 0) for t in range(4)]
        twist(63, r0 + ROOT * (r1 - r3), -r2 - ROOT * (r1 + r3))
        twist(64, r0 - ROOT * (r1 - r3), r2 - ROOT * (r1 + r3))

        def last(chunk):
            rows = pl.ds(multiple(chunk * 416, 16), 416)
            out = dot(zh[rows, :], mh[...]) + dot(zl[rows, :], mh[...]) + dot(zh[rows, :], ml[...])
            spec[pl.ds(chunk * 13, 13)] = out.reshape(13, 32, 256)

        unrolled(0, 5, last)

    def times(left, right, sign):
        lr, li = left[..., 0:128], left[..., 128:256] * sign
        rr, ri = right[..., 0:128], right[..., 128:256]
        return jnp.concatenate([lr * rr - li * ri, lr * ri + li * rr], axis=2)

    def inverse(product, count, store, more=None):
        size = 16 * count
        wide = 128 * count

        def first(chunk):
            high, low = halves(product(pl.ds(chunk * 13, 13)).reshape(13 * size, 256))
            rows = pl.ds(multiple(chunk * 13 * size, 16), 13 * size)
            e[rows, :] = dot(high, nh[...]) + dot(low, nh[...]) + dot(high, nl[...])

        unrolled(0, 5, first)

        def untwist(index):
            cos, sin = twc[pl.ds(index, 1), :][:, 0:wide], tws[pl.ds(index, 1), :][:, 0:wide]
            parts = [e[pl.ds(multiple(index * size + 16 * g, 16), 16), :] for g in range(count)]
            re = jnp.concatenate([p[:, 0:128] for p in parts], axis=1)
            im = jnp.concatenate([p[:, 128:256] for p in parts], axis=1)
            return re * cos - im * sin, im * cos + re * sin

        def store_w(tile, part, k1, value):
            rows = pl.ds(multiple(part * 256 + k1 * 16, 16), 16)
            high, low = halves(value)
            wh[tile, rows, 0:wide] = high
            wl[tile, rows, 0:wide] = low

        def butterfly(k1):
            base = (k1 - 1) * 4
            (r0, i0), (r1, i1), (r2, i2), (r3, i3) = [untwist(base + q) for q in range(4)]
            ar, ai, br, bi = r0 + r2, i0 + i2, r0 - r2, i0 - i2
            cr, ci, dr, di = r1 + r3, i1 + i3, r1 - r3, i1 - i3
            store_w(0, 0, k1, ar + cr)
            store_w(0, 1, k1, ai + ci)
            store_w(1, 0, k1, br - di)
            store_w(1, 1, k1, bi + dr)
            store_w(2, 0, k1, ar - cr)
            store_w(2, 1, k1, ai - ci)
            store_w(3, 0, k1, br + di)
            store_w(3, 1, k1, bi - dr)

        unrolled(1, 16, butterfly)
        (r0, _), (r32, i32), (r64, _), (r16, i16), (r48, i48) = [untwist(60 + n) for n in range(5)]
        plus, minus = 0.5 * (r0 + r64), 0.5 * (r0 - r64)
        store_w(0, 0, 0, plus + r32)
        store_w(1, 0, 0, minus - i32)
        store_w(2, 0, 0, plus - r32)
        store_w(3, 0, 0, minus + i32)
        store_w(0, 1, 0, r16 + r48)
        store_w(1, 1, 0, ROOT * (r16 - i16 - r48 - i48))
        store_w(2, 1, 0, i48 - i16)
        store_w(3, 1, 0, ROOT * (r48 - i48 - r16 - i16))

        def last(tile):
            high, low = wh[tile, :, 0:wide], wl[tile, :, 0:wide]
            out = dot(dh[tile], high) + dot(dh[tile], low) + dot(dl[tile], high)
            for g in range(count):
                store(g, tile, out[:, g * 128 : g * 128 + 128].astype(BF16).reshape(16, 16, 128))
            if more is not None and tile == 0:
                more(out)

        unrolled(0, 4, last)

    def filter_out():
        def product(index):
            return jnp.concatenate(
                [times(spec_p[h, index, 16:32, :], spec_p[h, index, 0:16, :], -1.0) for h in range(2)],
                axis=1)

        def store(g, tile, value):
            gf_s[:, g * 16 : g * 16 + 16, tile * 128 : tile * 128 + 128] = value

        inverse(product, 2, store)

        def one(n):
            chip = lax.rem(me // 2 + n, 8)

            @pl.when(2 * chip + half != me)
            def _():
                pltpu.make_async_remote_copy(
                    src_ref=gf_s.at[pl.ds(2 * chip, 2)], dst_ref=gf_r.at[me - 8 * half],
                    send_sem=send_sem.at[3], recv_sem=recv_sem.at[3],
                    device_id=(2 * chip + half, chan), device_id_type=MESH).start()

        loop(0, 8, one)

        @pl.when(core == half)
        def _():
            pltpu.make_async_copy(
                gf_s.at[pl.ds(2 * (me // 2), 2)], gf_r.at[me - 8 * half], recv_sem.at[3]).start()

    def mixes_out(h):
        def product(index):
            taps = spec_t[index, h * 16 : h * 16 + 16, :]
            return jnp.concatenate(
                [times(taps, spec_p[h, index, 16:32, :], 1.0), times(taps, spec_p[h, index, 0:16, :], -1.0)],
                axis=1)

        def store(g, tile, value):
            mm_s[h, :, 4 * g + tile] = value

        def more(out):
            mixed, grad_mix = out[16:256, 0:128], out[16:256, 128:256]
            side = lax.broadcasted_iota(jnp.int32, (240, 128), 1)
            value = jnp.where(side < 2, mixed, jnp.where(side < 4, pltpu.roll(grad_mix, 2, 1), pltpu.roll(grad_mix, 4, 1)))
            mm_s[h, 0:15, 8] = value.astype(BF16).reshape(15, 16, 128)
            mm_s[h, 15, 8] = jnp.zeros((16, 128), BF16)

        inverse(product, 2, store, more)
        send_all(4 + h, slot_of(mm_s.at[h]), mm_r.at[h])

    for n in range(6, 16):
        loads[n].wait()
    wait_bytes(taps_r, recv_sem.at[0])
    forward(lambda g, lanes: taps_r[:, g * 16 : g * 16 + 16, lanes], spec_t)
    for h in range(2):
        wait_bytes(pair_r.at[h], recv_sem.at[1 + h])
        forward(lambda g, lanes: pair_r[h, :, g, :, lanes], spec_p.at[h])
        if h == 1:
            filter_out()
        mixes_out(h)

    def adjoint(h, sums):
        wait_bytes(mm_r.at[h], recv_sem.at[4 + h])

        def body(block):
            rows = rows_of(block, h)
            weight = wcol[rows, :]
            skip = weight[:, 9:10]
            spot = pl.ds(multiple(block * 16, 16), 16)
            halo = head_mult[h, spot, :] * (mm_r[h, block, 8].astype(F32) + skip * head_gate[h, spot, :])
            mixed, grad_mix = [
                jnp.concatenate([mm_r[h, block, 4 * g + tile] for tile in range(4)], axis=1).astype(F32)
                + skip * pair_s[h, block, 1 - g].astype(F32)
                for g in range(2)
            ]
            fields = (go[rows, :].astype(F32) * mixed, grad_mix * actv[rows, :], grad_mix * act2[rows, :])
            total = jnp.zeros((16, 512), F32)
            for s, (field, stream, out) in enumerate(zip(fields, (x1, x2, xv), (o1, o2, ov))):
                next_one, next_two = halo[:, 2 * s : 2 * s + 1], halo[:, 2 * s + 1 : 2 * s + 2]
                one = jnp.where(lane16 == 511, next_one, pltpu.roll(field, 511, 1))
                two = jnp.where(
                    lane16 == 511, next_two, jnp.where(lane16 == 510, next_one, pltpu.roll(field, 510, 1)))
                full = (
                    weight[:, 3 * s : 3 * s + 1] * field
                    + weight[:, 3 * s + 1 : 3 * s + 2] * one
                    + weight[:, 3 * s + 2 : 3 * s + 3] * two
                )
                out[rows, :] = full.astype(BF16)
                total += stream[rows, :].astype(F32) * full
            return total[0:8] + total[8:16]

        for block in range(16):
            sums = sums + body(block)
        return sums

    loads[16].wait()
    swap_in = neighbour(sk_h, sk.at[1 - core], 2, sibling)
    swap_in.wait_recv()
    wait_bytes(gf_s, recv_sem.at[3])

    def sketch_rows(block):
        rows = pl.ds(block * 256, 256)
        total = dot_nt(sk[0, rows, :], gf_r[:, 0].reshape(256, 512))
        total += dot_nt(sk[1, rows, :], gf_r[:, 1].reshape(256, 512))
        part_s[pl.ds(block * 4, 4)] = total.astype(BF16).reshape(4, 64, 256)

    unrolled(0, 4, sketch_rows)
    send_all(6, slot_of(part_s), rs_r)
    head_copy.wait_recv()
    for h in range(2):
        heads = head_r[h].astype(F32) * (me < 15).astype(F32)
        wrow[0:16, 0:256] = heads
        head_gate[h] = jnp.transpose(wrow[:, 0:256])
        wrow[0:16, 0:256] = pltpu.roll(heads, 10, 0)
        head_mult[h] = jnp.transpose(wrow[:, 0:256])
    sal_s[...] = adjoint(1, adjoint(0, jnp.zeros((8, 512), F32)))
    outs = [
        pltpu.make_async_copy(a, b, out_sem.at[n])
        for n, (a, b) in enumerate(((o1, o1_h), (o2, o2_h), (ov, ov_h), (osk, osk_h), (osal, osal_h)))
    ]
    for n in range(3):
        outs[n].start()

    def sal_send_to(i):
        pltpu.make_async_remote_copy(
            src_ref=sal_s, dst_ref=sal_r.at[chan], send_sem=sal_send.at[0], recv_sem=sal_recv.at[0],
            device_id=(me, lax.rem(chan + i, 8)), device_id_type=MESH).start()

    loop(1, 8, sal_send_to)
    pltpu.make_async_copy(sal_s, sal_r.at[chan], sal_recv.at[0]).start()

    wait_bytes(rs_r, recv_sem.at[6])
    for side in range(2):
        total = rs_r[side].astype(F32)
        for chip in range(1, 8):
            total += rs_r[2 * chip + side].astype(F32)
        osk[:, side * 256 : side * 256 + 256] = total
    outs[3].start()

    wait_bytes(sal_r, sal_recv.at[0])
    total = sal_r[0]
    for n in range(1, 8):
        total += sal_r[n]
    total = jnp.sum(total, axis=0, keepdims=True) * (3.0 * D) ** (-0.5)
    total = jnp.broadcast_to(total, (8, 512))
    osal[...] = pltpu.roll(total, 512 - chan * 64, 1)[:, 0:128]
    outs[4].start()

    tail_copy.wait_send()
    swap.wait_send()
    head_copy.wait_send()
    wait_bytes(taps_r.at[pl.ds(0, 15)], send_sem.at[0])
    for h in range(2):
        wait_bytes(pair_s.at[h, pl.ds(0, 15)], send_sem.at[1 + h])
        wait_bytes(mm_s.at[h, pl.ds(0, 15)], send_sem.at[4 + h])
    wait_bytes(gf_s.at[pl.ds(0, 14)], send_sem.at[3])

    @pl.when(core != half)
    def _():
        wait_bytes(gf_s.at[pl.ds(14, 2)], send_sem.at[3])

    wait_bytes(part_s.at[pl.ds(0, 15)], send_sem.at[6])
    wait_bytes(sal_r.at[pl.ds(0, 7)], sal_send.at[0])
    for out in outs:
        out.wait()


def finish(a1, a2, av, asal, ask, b1, b2, bv, bsal, bsk, c1, c2, cv, ck, in_sem, out_sem):
    stages = ((a1, c1, b1), (a2, c2, b2), (av, cv, bv), (ask, ck, bsk))
    ins = [pltpu.make_async_copy(a, c, in_sem.at[n]) for n, (a, c, _) in enumerate(stages)]
    outs = [pltpu.make_async_copy(c, b, out_sem.at[n]) for n, (_, c, b) in enumerate(stages)]
    for copy in ins:
        copy.start()
    bsal[...] = asal[0, 0:64]
    for first, second in zip(ins, outs):
        first.wait()
        second.start()
    for copy in outs:
        copy.wait()


def on_device(*arrays):
    one, two, value, grad, taps, short, gain, sketch = arrays
    tables = [jnp.asarray(t) for t in host_tables()]
    operands = [one, two, value, grad, taps, short, gain.reshape(1, 512), sketch] + tables

    def vmem(shape, dtype=BF16):
        return pltpu.VMEM(shape, dtype)

    square = (512, 512)
    parts = (2, 16, 2, 16, 512)
    mixes = (2, 16, 9, 16, 128)
    scratch = [
        *[vmem(square) for _ in range(4)], vmem((3, 3, 512), F32), vmem((1, 512), F32), vmem((2, 1024, 512)),
        *[vmem(t.shape, t.dtype) for t in tables],
        vmem((128, 512), F32), vmem((512, 128), F32),
        vmem((16, 512)), vmem((16, 512)), vmem((2, 16, 256)), vmem((2, 16, 256)), vmem((512, 128), F32),
        vmem((2, 5, 256, 128)), vmem((2, 256, 128), F32), vmem((2, 256, 128), F32),
        vmem(square, F32), vmem(square, F32),
        vmem(parts), vmem(parts), vmem((16, 32, 512)),
        vmem((4, 512, 256), F32), vmem((ROWS, 256)), vmem((ROWS, 256)),
        vmem((65, 32, 256), F32), vmem((2, 65, 32, 256), F32), vmem((ROWS, 256), F32),
        vmem((4, 512, 256)), vmem((4, 512, 256)),
        vmem((16, 32, 512)), vmem((8, 2, 32, 512)), vmem(mixes), vmem(mixes),
        vmem((16, 64, 256)), vmem((16, 64, 256)),
        vmem((8, 512), F32), vmem((8, 8, 512), F32),
        *[vmem(square) for _ in range(3)], vmem((8, 128), F32), vmem((64, 512), F32),
        pltpu.SemaphoreType.DMA((17,)), pltpu.SemaphoreType.DMA((5,)),
        pltpu.SemaphoreType.DMA((7,)), pltpu.SemaphoreType.DMA((7,)),
        pltpu.SemaphoreType.DMA((3,)), pltpu.SemaphoreType.DMA((3,)),
        pltpu.SemaphoreType.DMA((1,)), pltpu.SemaphoreType.DMA((1,)),
    ]
    results = pl.pallas_call(
        kernel,
        out_shape=[
            *[jax.ShapeDtypeStruct(square, BF16) for _ in range(3)],
            jax.ShapeDtypeStruct((8, 128), F32),
            jax.ShapeDtypeStruct((64, 512), F32),
        ],
        in_specs=[pl.BlockSpec(memory_space=pl.ANY) for _ in operands],
        out_specs=[pl.BlockSpec(memory_space=pl.ANY) for _ in range(5)],
        scratch_shapes=scratch,
        compiler_params=pltpu.CompilerParams(
            collective_id=0, has_side_effects=True, vmem_limit_bytes=56 * 1024 * 1024),
    )(*operands)
    anywhere = pl.BlockSpec(memory_space=pl.ANY)
    near = pl.BlockSpec(memory_space=pltpu.VMEM)
    return pl.pallas_call(
        finish,
        out_shape=[
            *[jax.ShapeDtypeStruct(square, BF16) for _ in range(3)],
            jax.ShapeDtypeStruct((64,), F32),
            jax.ShapeDtypeStruct((64, 512), F32),
        ],
        in_specs=[anywhere, anywhere, anywhere, near, anywhere],
        out_specs=[anywhere, anywhere, anywhere, near, anywhere],
        scratch_shapes=[
            *[vmem(square) for _ in range(3)], vmem((64, 512), F32),
            pltpu.SemaphoreType.DMA((4,)), pltpu.SemaphoreType.DMA((4,)),
        ],
    )(*results)


def solution(mesh):
    return jax.shard_map(
        on_device,
        mesh=mesh,
        in_specs=(
            P("chan", "seq"),
            P("chan", "seq"),
            P("chan", "seq"),
            P("chan", "seq"),
            P("chan", "seq"),
            P(None, None, "chan"),
            P("chan"),
            P(None, "seq"),
        ),
        out_specs=(
            P("chan", "seq"),
            P("chan", "seq"),
            P("chan", "seq"),
            P(("seq", "chan")),
            P("seq", "chan"),
        ),
        check_vma=False,
    )
```

```python
import functools
import math

import jax
import jax.numpy as jnp
import numpy as np
from jax import lax
from jax.experimental import pallas as pl
from jax.experimental.pallas import tpu as pltpu
from jax.sharding import PartitionSpec as P

D = 4096
MESH = pl.DeviceIdType.MESH
F32 = jnp.float32
BF16 = jnp.bfloat16
ROOT = math.sqrt(0.5)
FREQS = [k1 + 32 * q for k1 in range(1, 16) for q in range(4)] + [0, 32, 64, 16, 48]
ROWS = 32 * len(FREQS)


def split_host(table):
    high = table.astype(jnp.bfloat16)
    low = (table - high.astype(np.float64)).astype(jnp.bfloat16)
    return high, low


def host_tables():
    shard = np.arange(16)
    k1 = np.arange(16)
    first = np.zeros((4, 32, 16))
    for tile in range(4):
        angle = 2 * np.pi * np.outer(k1, 4 * shard + tile) / 128
        first[tile, :16] = np.cos(angle)
        first[tile, 16:] = -np.sin(angle)
        first[tile, 16] = (-1.0) ** shard
    eye = np.eye(16)
    wide = np.einsum("tks,cd->tkcsd", first, eye).reshape(4, 512, 256)
    back = np.einsum("tks,cd->tsckd", first, eye).reshape(4, 256, 512) * (2.0 / 16384)
    lane = np.arange(128)
    angle = 2 * np.pi * np.outer(lane, lane) / 128
    cos, sin = np.cos(angle), np.sin(angle)
    inner = np.block([[cos, -sin], [sin, cos]])
    inner_back = np.block([[cos, sin], [-sin, cos]])
    twist = 2 * np.pi * np.outer(np.array(FREQS + [0] * 7), lane) / 16384
    twist = np.concatenate([twist, twist], axis=1)
    return (
        *split_host(wide),
        *split_host(back),
        *split_host(inner),
        *split_host(inner_back),
        np.cos(twist).astype(np.float32),
        np.sin(twist).astype(np.float32),
    )


def dot(left, right):
    return jnp.dot(left, right, preferred_element_type=F32)


def dot_nt(left, right):
    return lax.dot_general(left, right, (((1,), (1,)), ((), ())), preferred_element_type=F32)


def halves(value):
    high = value.astype(BF16)
    return high, (value - high.astype(F32)).astype(BF16)


def multiple(value, of):
    return value if isinstance(value, int) else pl.multiple_of(value, of)


def unrolled(first, last, body):
    for index in range(first, last):
        body(index)


def loop(first, last, body):
    def step(index, carry):
        body(index)
        return carry

    lax.fori_loop(first, last, step, 0)


def kernel(
    x1_h, x2_h, xv_h, go_h, taps_h, short_h, gain_h, sk_h,
    c1h_h, c1l_h, dh_h, dl_h, mh_h, ml_h, nh_h, nl_h, twc_h, tws_h,
    o1_h, o2_h, ov_h, osal_h, osk_h,
    x1, x2, xv, go, short, gain, sk,
    c1h, c1l, dh, dl, mh, ml, nh, nl, twc, tws,
    wrow, wcol, tail_s, tail_r, head_s, head_r, hcol, head_tile, head_gate, head_mult,
    act2, actv,
    pair_s, pair_r, taps_r,
    y, zh, zl, spec_t, spec_p, e, wh, wl,
    gf_s, gf_r, mm_s, mm_r,
    part_s, rs_r, sal_s, sal_r, o1, o2, ov, osal, osk,
    load_sem, out_sem, send_sem, recv_sem, halo_send, halo_recv, sal_send, sal_recv,
):
    me = lax.axis_index("seq")
    chan = lax.axis_index("chan")
    core = lax.rem(me, 2)
    half = me // 8
    sibling = me + 1 - 2 * core
    following = lax.rem(me + 1, 16)
    previous = lax.rem(me + 15, 16)

    loads = [
        (x1_h, x1), (x2_h, x2), (xv_h, xv), (go_h, go), (short_h, short), (gain_h, gain),
        (c1h_h, c1h), (c1l_h, c1l), (mh_h, mh), (ml_h, ml), (twc_h, twc), (tws_h, tws),
        (nh_h, nh), (nl_h, nl), (dh_h, dh), (dl_h, dl), (sk_h, sk.at[core]),
    ]
    loads = [pltpu.make_async_copy(a, b, load_sem.at[n]) for n, (a, b) in enumerate(loads)]
    for load in loads:
        load.start()

    barrier = pltpu.get_barrier_semaphore()
    loop(1, 16, lambda i: pl.semaphore_signal(
        barrier, inc=1, device_id=(lax.rem(me + i, 16), chan), device_id_type=MESH))
    loop(1, 8, lambda i: pl.semaphore_signal(
        barrier, inc=1, device_id=(me, lax.rem(chan + i, 8)), device_id_type=MESH))

    def block_of(ref):
        return lambda to: ref.at[pl.ds(multiple(to * 32, 32), 32)]

    def slot_of(ref):
        return lambda to: ref.at[to]

    def send_all(kind, source, target):
        def one(i):
            to = lax.rem(me + i, 16)
            pltpu.make_async_remote_copy(
                src_ref=source(to), dst_ref=target.at[me],
                send_sem=send_sem.at[kind], recv_sem=recv_sem.at[kind],
                device_id=(to, chan), device_id_type=MESH,
            ).start()

        loop(1, 16, one)
        pltpu.make_async_copy(source(me), target.at[me], recv_sem.at[kind]).start()

    def wait_bytes(ref, sem):
        pltpu.make_async_copy(ref, ref, sem).wait()

    def neighbour(source, target, n, to):
        return pltpu.make_async_remote_copy(
            src_ref=source, dst_ref=target, send_sem=halo_send.at[n], recv_sem=halo_recv.at[n],
            device_id=(to, chan), device_id_type=MESH)

    for n in range(3):
        loads[n].wait()
    row = lax.broadcasted_iota(jnp.int32, (16, 128), 0)
    lane = lax.broadcasted_iota(jnp.int32, (16, 128), 1)
    tails = jnp.zeros((16, 512), F32)
    for s, ref in enumerate((x1, x2, xv)):
        pick = ((row == 2 * s) & (lane == 126)) | ((row == 2 * s + 1) & (lane == 127))
        tails += dot_nt(pick.astype(F32).astype(BF16), ref[:, 384:512])
    tail_s[...] = tails.astype(BF16)

    pl.semaphore_wait(barrier, 22)
    tail_copy = neighbour(tail_s, tail_r, 0, following)
    tail_copy.start()
    send_all(0, block_of(taps_h), taps_r)
    for n in range(3, 6):
        loads[n].wait()

    wrow[...] = jnp.zeros((128, 512), F32)
    for s in range(3):
        wrow[3 * s : 3 * s + 3, :] = short[s]
    wrow[9:10, :] = gain[...]
    wcol[...] = jnp.transpose(wrow[...])

    tail_copy.wait_recv()
    wrow[0:16, :] = tail_r[...].astype(F32) * (me > 0).astype(F32)
    hcol[...] = jnp.transpose(wrow[...])

    lane16 = lax.broadcasted_iota(jnp.int32, (16, 512), 1)

    def rows_of(block, h):
        return pl.ds(multiple(block * 32 + h * 16, 16), 16)

    def gate(h):
        def body(block):
            rows = rows_of(block, h)
            weight = wcol[rows, :]
            halo = hcol[rows, :]

            def short_filter(ref, s):
                field = ref[rows, :].astype(F32)
                before, last = halo[:, 2 * s : 2 * s + 1], halo[:, 2 * s + 1 : 2 * s + 2]
                one = jnp.where(lane16 == 0, last, pltpu.roll(field, 1, 1))
                two = jnp.where(lane16 == 0, before, jnp.where(lane16 == 1, last, pltpu.roll(field, 2, 1)))
                return (
                    weight[:, 3 * s : 3 * s + 1] * field
                    + weight[:, 3 * s + 1 : 3 * s + 2] * one
                    + weight[:, 3 * s + 2 : 3 * s + 3] * two
                )

            first = short_filter(x1, 0)
            grad = go[rows, :]
            grad_gate = (grad.astype(F32) * first).astype(BF16)
            pair_s[h, block, 0] = grad_gate
            second = short_filter(x2, 1)
            value = short_filter(xv, 2)
            act2[rows, :] = second
            actv[rows, :] = value
            gated = (second * value).astype(BF16)
            pair_s[h, block, 1] = gated
            spot = pl.ds(multiple(block * 16, 16), 16)
            head_tile[h, 0, spot, :] = gated[:, 0:128]
            head_tile[h, 1, spot, :] = grad_gate[:, 0:128]
            head_tile[h, 2, spot, :] = grad[:, 0:128]
            head_tile[h, 3, spot, :] = value[:, 0:128].astype(BF16)
            head_tile[h, 4, spot, :] = second[:, 0:128].astype(BF16)

        unrolled(0, 16, body)

    for h in range(2):
        gate(h)
        send_all(1 + h, slot_of(pair_s.at[h]), pair_r.at[h])
    swap = neighbour(sk_h, sk.at[core], 2, sibling)
    swap.start()

    for h in range(2):
        heads = jnp.zeros((16, 256), F32)
        for at, n in ((0, 0), (2, 1), (4, 1), (6, 2), (8, 3), (10, 4)):
            pick = ((row == at) & (lane == 0)) | ((row == at + 1) & (lane == 1))
            heads += dot_nt(pick.astype(F32).astype(BF16), head_tile[h, n])
        head_s[h] = heads.astype(BF16)
    head_copy = neighbour(head_s, head_r, 1, previous)
    head_copy.start()

    def first_rows(tile, part, k1):
        return y[tile, pl.ds(multiple(part * 256 + k1 * 16, 16), 16), :]

    def store_z(index, re, im):
        for g in range(2):
            rows = pl.ds(multiple(index * 32 + g * 16, 16), 16)
            side = slice(g * 128, g * 128 + 128)
            high, low = halves(jnp.concatenate([re[:, side], im[:, side]], axis=1))
            zh[rows, :] = high
            zl[rows, :] = low

    def twist(index, re, im):
        cos, sin = twc[pl.ds(index, 1), :], tws[pl.ds(index, 1), :]
        store_z(index, re * cos + im * sin, im * cos - re * sin)

    def forward(source, spec):
        def stage(tile):
            lanes = pl.ds(multiple(tile * 128, 128), 128)
            right = jnp.concatenate([source(g, lanes).reshape(256, 128) for g in range(2)], axis=1)
            y[tile] = dot(c1h[tile], right) + dot(c1l[tile], right)

        unrolled(0, 4, stage)

        def butterfly(k1):
            r0, r1, r2, r3 = [first_rows(t, 0, k1) for t in range(4)]
            i0, i1, i2, i3 = [first_rows(t, 1, k1) for t in range(4)]
            ar, ai, br, bi = r0 + r2, i0 + i2, r0 - r2, i0 - i2
            cr, ci, dr, di = r1 + r3, i1 + i3, r1 - r3, i1 - i3
            base = (k1 - 1) * 4
            twist(base, ar + cr, ai + ci)
            twist(base + 1, br + di, bi - dr)
            twist(base + 2, ar - cr, ai - ci)
            twist(base + 3, br - di, bi + dr)

        unrolled(1, 16, butterfly)
        r0, r1, r2, r3 = [first_rows(t, 0, 0) for t in range(4)]
        none = jnp.zeros_like(r0)
        store_z(60, r0 + r1 + r2 + r3, none)
        twist(61, r0 - r2, r3 - r1)
        twist(62, r0 - r1 + r2 - r3, none)
        r0, r1, r2, r3 = [first_rows(t, 1, 0) for t in range(4)]
        twist(63, r0 + ROOT * (r1 - r3), -r2 - ROOT * (r1 + r3))
        twist(64, r0 - ROOT * (r1 - r3), r2 - ROOT * (r1 + r3))

        def last(chunk):
            rows = pl.ds(multiple(chunk * 416, 16), 416)
            out = dot(zh[rows, :], mh[...]) + dot(zl[rows, :], mh[...]) + dot(zh[rows, :], ml[...])
            spec[pl.ds(chunk * 13, 13)] = out.reshape(13, 32, 256)

        unrolled(0, 5, last)

    def times(left, right, sign):
        lr, li = left[..., 0:128], left[..., 128:256] * sign
        rr, ri = right[..., 0:128], right[..., 128:256]
        return jnp.concatenate([lr * rr - li * ri, lr * ri + li * rr], axis=2)

    def inverse(product, count, store, more=None):
        size = 16 * count
        wide = 128 * count

        def first(chunk):
            high, low = halves(product(pl.ds(chunk * 13, 13)).reshape(13 * size, 256))
            rows = pl.ds(multiple(chunk * 13 * size, 16), 13 * size)
            e[rows, :] = dot(high, nh[...]) + dot(low, nh[...]) + dot(high, nl[...])

        unrolled(0, 5, first)

        def untwist(index):
            cos, sin = twc[pl.ds(index, 1), :][:, 0:wide], tws[pl.ds(index, 1), :][:, 0:wide]
            parts = [e[pl.ds(multiple(index * size + 16 * g, 16), 16), :] for g in range(count)]
            re = jnp.concatenate([p[:, 0:128] for p in parts], axis=1)
            im = jnp.concatenate([p[:, 128:256] for p in parts], axis=1)
            return re * cos - im * sin, im * cos + re * sin

        def store_w(tile, part, k1, value):
            rows = pl.ds(multiple(part * 256 + k1 * 16, 16), 16)
            high, low = halves(value)
            wh[tile, rows, 0:wide] = high
            wl[tile, rows, 0:wide] = low

        def butterfly(k1):
            base = (k1 - 1) * 4
            (r0, i0), (r1, i1), (r2, i2), (r3, i3) = [untwist(base + q) for q in range(4)]
            ar, ai, br, bi = r0 + r2, i0 + i2, r0 - r2, i0 - i2
            cr, ci, dr, di = r1 + r3, i1 + i3, r1 - r3, i1 - i3
            store_w(0, 0, k1, ar + cr)
            store_w(0, 1, k1, ai + ci)
            store_w(1, 0, k1, br - di)
            store_w(1, 1, k1, bi + dr)
            store_w(2, 0, k1, ar - cr)
            store_w(2, 1, k1, ai - ci)
            store_w(3, 0, k1, br + di)
            store_w(3, 1, k1, bi - dr)

        unrolled(1, 16, butterfly)
        (r0, _), (r32, i32), (r64, _), (r16, i16), (r48, i48) = [untwist(60 + n) for n in range(5)]
        plus, minus = 0.5 * (r0 + r64), 0.5 * (r0 - r64)
        store_w(0, 0, 0, plus + r32)
        store_w(1, 0, 0, minus - i32)
        store_w(2, 0, 0, plus - r32)
        store_w(3, 0, 0, minus + i32)
        store_w(0, 1, 0, r16 + r48)
        store_w(1, 1, 0, ROOT * (r16 - i16 - r48 - i48))
        store_w(2, 1, 0, i48 - i16)
        store_w(3, 1, 0, ROOT * (r48 - i48 - r16 - i16))

        def last(tile):
            high, low = wh[tile, :, 0:wide], wl[tile, :, 0:wide]
            out = dot(dh[tile], high) + dot(dh[tile], low) + dot(dl[tile], high)
            for g in range(count):
                store(g, tile, out[:, g * 128 : g * 128 + 128].astype(BF16).reshape(16, 16, 128))
            if more is not None and tile == 0:
                more(out)

        unrolled(0, 4, last)

    def filter_out():
        def product(index):
            return jnp.concatenate(
                [times(spec_p[h, index, 16:32, :], spec_p[h, index, 0:16, :], -1.0) for h in range(2)],
                axis=1)

        def store(g, tile, value):
            gf_s[:, g * 16 : g * 16 + 16, tile * 128 : tile * 128 + 128] = value

        inverse(product, 2, store)

        def one(n):
            chip = lax.rem(me // 2 + n, 8)

            @pl.when(2 * chip + half != me)
            def _():
                pltpu.make_async_remote_copy(
                    src_ref=gf_s.at[pl.ds(2 * chip, 2)], dst_ref=gf_r.at[me - 8 * half],
                    send_sem=send_sem.at[3], recv_sem=recv_sem.at[3],
                    device_id=(2 * chip + half, chan), device_id_type=MESH).start()

        loop(0, 8, one)

        @pl.when(core == half)
        def _():
            pltpu.make_async_copy(
                gf_s.at[pl.ds(2 * (me // 2), 2)], gf_r.at[me - 8 * half], recv_sem.at[3]).start()

    def mixes_out(h):
        def product(index):
            taps = spec_t[index, h * 16 : h * 16 + 16, :]
            return jnp.concatenate(
                [times(taps, spec_p[h, index, 16:32, :], 1.0), times(taps, spec_p[h, index, 0:16, :], -1.0)],
                axis=1)

        def store(g, tile, value):
            mm_s[h, :, 4 * g + tile] = value

        def more(out):
            mixed, grad_mix = out[16:256, 0:128], out[16:256, 128:256]
            side = lax.broadcasted_iota(jnp.int32, (240, 128), 1)
            value = jnp.where(side < 2, mixed, jnp.where(side < 4, pltpu.roll(grad_mix, 2, 1), pltpu.roll(grad_mix, 4, 1)))
            mm_s[h, 0:15, 8] = value.astype(BF16).reshape(15, 16, 128)
            mm_s[h, 15, 8] = jnp.zeros((16, 128), BF16)

        inverse(product, 2, store, more)
        send_all(4 + h, slot_of(mm_s.at[h]), mm_r.at[h])

    for n in range(6, 16):
        loads[n].wait()
    wait_bytes(taps_r, recv_sem.at[0])
    forward(lambda g, lanes: taps_r[:, g * 16 : g * 16 + 16, lanes], spec_t)
    for h in range(2):
        wait_bytes(pair_r.at[h], recv_sem.at[1 + h])
        forward(lambda g, lanes: pair_r[h, :, g, :, lanes], spec_p.at[h])
        if h == 1:
            filter_out()
        mixes_out(h)

    def adjoint(h, sums):
        wait_bytes(mm_r.at[h], recv_sem.at[4 + h])

        def body(block):
            rows = rows_of(block, h)
            weight = wcol[rows, :]
            skip = weight[:, 9:10]
            spot = pl.ds(multiple(block * 16, 16), 16)
            halo = head_mult[h, spot, :] * (mm_r[h, block, 8].astype(F32) + skip * head_gate[h, spot, :])
            mixed, grad_mix = [
                jnp.concatenate([mm_r[h, block, 4 * g + tile] for tile in range(4)], axis=1).astype(F32)
                + skip * pair_s[h, block, 1 - g].astype(F32)
                for g in range(2)
            ]
            fields = (go[rows, :].astype(F32) * mixed, grad_mix * actv[rows, :], grad_mix * act2[rows, :])
            total = jnp.zeros((16, 512), F32)
            for s, (field, stream, out) in enumerate(zip(fields, (x1, x2, xv), (o1, o2, ov))):
                next_one, next_two = halo[:, 2 * s : 2 * s + 1], halo[:, 2 * s + 1 : 2 * s + 2]
                one = jnp.where(lane16 == 511, next_one, pltpu.roll(field, 511, 1))
                two = jnp.where(
                    lane16 == 511, next_two, jnp.where(lane16 == 510, next_one, pltpu.roll(field, 510, 1)))
                full = (
                    weight[:, 3 * s : 3 * s + 1] * field
                    + weight[:, 3 * s + 1 : 3 * s + 2] * one
                    + weight[:, 3 * s + 2 : 3 * s + 3] * two
                )
                out[rows, :] = full.astype(BF16)
                total += stream[rows, :].astype(F32) * full
            return total[0:8] + total[8:16]

        for block in range(16):
            sums = sums + body(block)
        return sums

    head_copy.wait_recv()
    for h in range(2):
        heads = head_r[h].astype(F32) * (me < 15).astype(F32)
        wrow[0:16, 0:256] = heads
        head_gate[h] = jnp.transpose(wrow[:, 0:256])
        wrow[0:16, 0:256] = pltpu.roll(heads, 10, 0)
        head_mult[h] = jnp.transpose(wrow[:, 0:256])
    sums = adjoint(0, jnp.zeros((8, 512), F32))

    loads[16].wait()
    swap_in = neighbour(sk_h, sk.at[1 - core], 2, sibling)
    swap_in.wait_recv()
    wait_bytes(gf_s, recv_sem.at[3])

    def sketch_rows(block):
        rows = pl.ds(block * 256, 256)
        total = dot_nt(sk[0, rows, :], gf_r[:, 0].reshape(256, 512))
        total += dot_nt(sk[1, rows, :], gf_r[:, 1].reshape(256, 512))
        part_s[pl.ds(block * 4, 4)] = total.astype(BF16).reshape(4, 64, 256)

    unrolled(0, 4, sketch_rows)
    send_all(6, slot_of(part_s), rs_r)
    sal_s[...] = adjoint(1, sums)
    outs = [
        pltpu.make_async_copy(a, b, out_sem.at[n])
        for n, (a, b) in enumerate(((o1, o1_h), (o2, o2_h), (ov, ov_h), (osk, osk_h), (osal, osal_h)))
    ]
    for n in range(3):
        outs[n].start()

    def sal_send_to(i):
        pltpu.make_async_remote_copy(
            src_ref=sal_s, dst_ref=sal_r.at[chan], send_sem=sal_send.at[0], recv_sem=sal_recv.at[0],
            device_id=(me, lax.rem(chan + i, 8)), device_id_type=MESH).start()

    loop(1, 8, sal_send_to)
    pltpu.make_async_copy(sal_s, sal_r.at[chan], sal_recv.at[0]).start()

    wait_bytes(rs_r, recv_sem.at[6])
    for side in range(2):
        total = rs_r[side].astype(F32)
        for chip in range(1, 8):
            total += rs_r[2 * chip + side].astype(F32)
        osk[:, side * 256 : side * 256 + 256] = total
    outs[3].start()

    wait_bytes(sal_r, sal_recv.at[0])
    total = sal_r[0]
    for n in range(1, 8):
        total += sal_r[n]
    total = jnp.sum(total, axis=0, keepdims=True) * (3.0 * D) ** (-0.5)
    total = jnp.broadcast_to(total, (8, 512))
    osal[...] = pltpu.roll(total, 512 - chan * 64, 1)[:, 0:128]
    outs[4].start()

    tail_copy.wait_send()
    swap.wait_send()
    head_copy.wait_send()
    wait_bytes(taps_r.at[pl.ds(0, 15)], send_sem.at[0])
    for h in range(2):
        wait_bytes(pair_s.at[h, pl.ds(0, 15)], send_sem.at[1 + h])
        wait_bytes(mm_s.at[h, pl.ds(0, 15)], send_sem.at[4 + h])
    wait_bytes(gf_s.at[pl.ds(0, 14)], send_sem.at[3])

    @pl.when(core != half)
    def _():
        wait_bytes(gf_s.at[pl.ds(14, 2)], send_sem.at[3])

    wait_bytes(part_s.at[pl.ds(0, 15)], send_sem.at[6])
    wait_bytes(sal_r.at[pl.ds(0, 7)], sal_send.at[0])
    for out in outs:
        out.wait()


def finish(a1, a2, av, asal, ask, b1, b2, bv, bsal, bsk, c1, c2, cv, ck, in_sem, out_sem):
    stages = ((a1, c1, b1), (a2, c2, b2), (av, cv, bv), (ask, ck, bsk))
    ins = [pltpu.make_async_copy(a, c, in_sem.at[n]) for n, (a, c, _) in enumerate(stages)]
    outs = [pltpu.make_async_copy(c, b, out_sem.at[n]) for n, (_, c, b) in enumerate(stages)]
    for copy in ins:
        copy.start()
    bsal[...] = asal[0, 0:64]
    for first, second in zip(ins, outs):
        first.wait()
        second.start()
    for copy in outs:
        copy.wait()


def on_device(*arrays):
    one, two, value, grad, taps, short, gain, sketch = arrays
    tables = [jnp.asarray(t) for t in host_tables()]
    operands = [one, two, value, grad, taps, short, gain.reshape(1, 512), sketch] + tables

    def vmem(shape, dtype=BF16):
        return pltpu.VMEM(shape, dtype)

    square = (512, 512)
    parts = (2, 16, 2, 16, 512)
    mixes = (2, 16, 9, 16, 128)
    scratch = [
        *[vmem(square) for _ in range(4)], vmem((3, 3, 512), F32), vmem((1, 512), F32), vmem((2, 1024, 512)),
        *[vmem(t.shape, t.dtype) for t in tables],
        vmem((128, 512), F32), vmem((512, 128), F32),
        vmem((16, 512)), vmem((16, 512)), vmem((2, 16, 256)), vmem((2, 16, 256)), vmem((512, 128), F32),
        vmem((2, 5, 256, 128)), vmem((2, 256, 128), F32), vmem((2, 256, 128), F32),
        vmem(square, F32), vmem(square, F32),
        vmem(parts), vmem(parts), vmem((16, 32, 512)),
        vmem((4, 512, 256), F32), vmem((ROWS, 256)), vmem((ROWS, 256)),
        vmem((65, 32, 256), F32), vmem((2, 65, 32, 256), F32), vmem((ROWS, 256), F32),
        vmem((4, 512, 256)), vmem((4, 512, 256)),
        vmem((16, 32, 512)), vmem((8, 2, 32, 512)), vmem(mixes), vmem(mixes),
        vmem((16, 64, 256)), vmem((16, 64, 256)),
        vmem((8, 512), F32), vmem((8, 8, 512), F32),
        *[vmem(square) for _ in range(3)], vmem((8, 128), F32), vmem((64, 512), F32),
        pltpu.SemaphoreType.DMA((17,)), pltpu.SemaphoreType.DMA((5,)),
        pltpu.SemaphoreType.DMA((7,)), pltpu.SemaphoreType.DMA((7,)),
        pltpu.SemaphoreType.DMA((3,)), pltpu.SemaphoreType.DMA((3,)),
        pltpu.SemaphoreType.DMA((1,)), pltpu.SemaphoreType.DMA((1,)),
    ]
    results = pl.pallas_call(
        kernel,
        out_shape=[
            *[jax.ShapeDtypeStruct(square, BF16) for _ in range(3)],
            jax.ShapeDtypeStruct((8, 128), F32),
            jax.ShapeDtypeStruct((64, 512), F32),
        ],
        in_specs=[pl.BlockSpec(memory_space=pl.ANY) for _ in operands],
        out_specs=[pl.BlockSpec(memory_space=pl.ANY) for _ in range(5)],
        scratch_shapes=scratch,
        compiler_params=pltpu.CompilerParams(
            collective_id=0, has_side_effects=True, vmem_limit_bytes=56 * 1024 * 1024),
    )(*operands)
    anywhere = pl.BlockSpec(memory_space=pl.ANY)
    near = pl.BlockSpec(memory_space=pltpu.VMEM)
    return pl.pallas_call(
        finish,
        out_shape=[
            *[jax.ShapeDtypeStruct(square, BF16) for _ in range(3)],
            jax.ShapeDtypeStruct((64,), F32),
            jax.ShapeDtypeStruct((64, 512), F32),
        ],
        in_specs=[anywhere, anywhere, anywhere, near, anywhere],
        out_specs=[anywhere, anywhere, anywhere, near, anywhere],
        scratch_shapes=[
            *[vmem(square) for _ in range(3)], vmem((64, 512), F32),
            pltpu.SemaphoreType.DMA((4,)), pltpu.SemaphoreType.DMA((4,)),
        ],
    )(*results)


def solution(mesh):
    return jax.shard_map(
        on_device,
        mesh=mesh,
        in_specs=(
            P("chan", "seq"),
            P("chan", "seq"),
            P("chan", "seq"),
            P("chan", "seq"),
            P("chan", "seq"),
            P(None, None, "chan"),
            P("chan"),
            P(None, "seq"),
        ),
        out_specs=(
            P("chan", "seq"),
            P("chan", "seq"),
            P("chan", "seq"),
            P(("seq", "chan")),
            P("seq", "chan"),
        ),
        check_vma=False,
    )
```
